32 devices in a mesh: ta: 4 (over z), gz: 4 (over y, core), gy: 2 (over x).
Axes of the slice: x: 2, y: 2, z: 4, core: 2. Of those that a mesh axis runs over, the one named last changes fastest.
Arguments:
- source: float32 [2, 4, 3, 16, 16, 256], P(None, None, None, 'ta', 'gz', 'gy'), may hold values from -6 to 6
- gauge_links: float32 [4, 2, 3, 3, 16, 16, 256], P(None, None, None, None, 'ta', 'gz', 'gy'), may hold values from -1 to 1, as said below
- near_null: bfloat16 [24, 2, 4, 3, 16, 16, 256], P(None, None, None, None, 'ta', 'gz', 'gy'), may hold values from -0.109375 to 0.109375
- w_first: float32 [9, 2, 1, 2, 4, 4], replicated, may hold values from -0.75 to 0.75
- w_second: float32 [9, 1, 2, 2, 4, 4], replicated, may hold values from -0.5 to 0.5
Outputs:
- network_out: float32 [2, 4, 3, 16, 16, 256], P(None, None, None, 'ta', 'gz', 'gy')
- coarse: float32 [2, 24, 4, 4, 16], P(None, None, 'ta', 'gz', 'gy')
- grad_first: float32 [9, 2, 1, 2, 4, 4], replicated
- grad_second: float32 [9, 1, 2, 2, 4, 4], replicated
The draws below stay inside these ranges and needn't reach their ends.
Inputs may be any that keep to these rules, and one draw needn't show every extreme that they name: `gauge_links`: every site's four link matrices are unitary 3 x 3 complex matrices of determinant one.
All inputs are finite; a program needn't handle non-finite values.
Results may differ from the reference program's by a relative error of at most 0.0003.
Values sent between devices are 32-bit elements; how exact they have to be, the bound alone decides.
A program may use at most 128 MiB of HBM per device.

```python
import math
import jax
import jax.numpy as jnp
import numpy as np
from jax import lax

BLK = 4
NNULL = 24
HID = 2
PATHS = 9
LX = 32
NT = 16
NZ = 16
NY = 8
NYX = 256


def rotation(theta, phase, lower_index, upper_index):
    filled = jnp.ones_like(theta)
    naught = jnp.zeros_like(theta)
    real_rows = [[filled if row_index == column else naught for column in range(3)] for row_index in range(3)]
    imag_rows = [[naught for column in range(3)] for row_index in range(3)]
    cosine = jnp.cos(theta)
    sine_part = jnp.sin(theta)
    real_rows[lower_index][lower_index] = cosine
    real_rows[upper_index][upper_index] = cosine
    real_rows[lower_index][upper_index] = -jnp.cos(phase) * sine_part
    imag_rows[lower_index][upper_index] = jnp.sin(phase) * sine_part
    real_rows[upper_index][lower_index] = jnp.cos(phase) * sine_part
    imag_rows[upper_index][lower_index] = jnp.sin(phase) * sine_part
    return (real_rows, imag_rows)


def complex_product(left_matrix, right_matrix):
    left_re, left_im = left_matrix
    right_re, right_im = right_matrix
    real_rows = []
    imag_rows = []
    for row_index in range(3):
        real_line = []
        imag_line = []
        for column in range(3):
            real_acc = left_re[row_index][0] * right_re[0][column] - left_im[row_index][0] * right_im[0][column]
            imag_acc = left_re[row_index][0] * right_im[0][column] + left_im[row_index][0] * right_re[0][column]
            for middle in range(1, 3):
                real_acc = real_acc + left_re[row_index][middle] * right_re[middle][column] - left_im[row_index][middle] * right_im[middle][column]
                imag_acc = imag_acc + left_re[row_index][middle] * right_im[middle][column] + left_im[row_index][middle] * right_re[middle][column]
            real_line.append(real_acc)
            imag_line.append(imag_acc)
        real_rows.append(real_line)
        imag_rows.append(imag_line)
    return (real_rows, imag_rows)


def draw_gauge_links(key, part):
    key = jax.random.fold_in(key, 11)
    angles = jax.random.uniform(key, (8, 4, NT, NZ, NYX), jnp.float32, -math.pi, math.pi)
    phase_one = angles[0]
    phase_two = angles[1]
    phase_three = -(phase_one + phase_two)
    naught = jnp.zeros_like(phase_one)
    diagonal_re = [[jnp.cos(phase_one), naught, naught], [naught, jnp.cos(phase_two), naught], [naught, naught, jnp.cos(phase_three)]]
    diagonal_im = [[jnp.sin(phase_one), naught, naught], [naught, jnp.sin(phase_two), naught], [naught, naught, jnp.sin(phase_three)]]
    matrix = (diagonal_re, diagonal_im)
    matrix = complex_product(matrix, rotation(angles[2], angles[3], 0, 1))
    matrix = complex_product(matrix, rotation(angles[4], angles[5], 1, 2))
    matrix = complex_product(matrix, rotation(angles[6], angles[7], 0, 2))
    real_part = jnp.stack([jnp.stack(row_values) for row_values in matrix[0]])
    imag_part = jnp.stack([jnp.stack(row_values) for row_values in matrix[1]])
    return jnp.transpose(jnp.stack([real_part, imag_part]), (3, 0, 1, 2, 4, 5, 6))


def level_of(key, extent, cuts, smallest, largest):
    loudness = 1.0
    for dim, parts in cuts:
        draws = jax.random.uniform(jax.random.fold_in(jax.random.fold_in(key, 6), dim), (parts,), jnp.float32, smallest / len(cuts), largest / len(cuts))
        loudness = loudness * jnp.repeat(jnp.exp(draws), extent[dim] // parts).reshape((-1,) + (1,) * (len(extent) - 1 - dim))
    return loudness


def normal_values(own_key, dims, scale, reach, shards=(), kind=jnp.bfloat16):
    result = jax.random.normal(own_key, dims, jnp.float32) * scale
    if len(shards) > 0:
        result = level_of(own_key, dims, shards, -0.22, 0.18) * result
    return jnp.clip(result, min=-reach, max=reach).astype(kind)


def setup_inputs(seed: int = 0) -> dict:
    key_list = jax.random.split(jax.random.key(seed), 6)
    return {
        "source": normal_values(key_list[0], (2, 4, 3, NT, NZ, NYX), 1.0, 6.0, ((3, 4), (4, 4), (5, 2)), jnp.float32),
        "gauge_links": draw_gauge_links(jax.random.fold_in(key_list[5], 71), 0),
        "near_null": normal_values(key_list[2], (NNULL, 2, 4, 3, NT, NZ, NYX), (12 * BLK * BLK * BLK * BLK) ** -0.5, 0.109375, ((4, 4), (5, 4), (6, 2))),
        "w_first": normal_values(key_list[3], (PATHS, HID, 1, 2, 4, 4), (8 * PATHS) ** -0.5, 0.75, (), jnp.float32),
        "w_second": normal_values(key_list[4], (PATHS, 1, HID, 2, 4, 4), (8 * PATHS * HID) ** -0.5, 0.5, (), jnp.float32),
    }


BARE_MASS = -0.5
HIGHEST_PRECISION = lax.Precision.HIGHEST

def spin_blocks():
    paulis = [np.array([[0, 1], [1, 0]], dtype=complex), np.array([[0, -1j], [1j, 0]], dtype=complex), np.array([[1, 0], [0, -1]], dtype=complex)]
    return [-1j * matrix for matrix in paulis] + [np.eye(2, dtype=complex)]

def projector_tables(parity):
    tables = []
    for corner in spin_blocks():
        dirac_gamma = np.zeros((4, 4), dtype=complex)
        dirac_gamma[:2, 2:] = corner
        dirac_gamma[2:, :2] = corner.conj().T
        tables.append(np.eye(4) + parity * dirac_gamma)
    stacked = np.stack(tables)
    return (jnp.asarray(stacked.real, jnp.float32), jnp.asarray(stacked.imag, jnp.float32))

def spin_apply(matrix_re, matrix_im, spinor):
    spinor_re = spinor[:, 0]
    spinor_im = spinor[:, 1]

    def contract(matrix, values):
        return jnp.einsum('ij,fjcabd->ficabd', matrix, values, precision=HIGHEST_PRECISION)
    out_re = contract(matrix_re, spinor_re) - contract(matrix_im, spinor_im)
    out_im = contract(matrix_re, spinor_im) + contract(matrix_im, spinor_re)
    return jnp.stack([out_re, out_im], axis=1)

def color_apply(link_field, spinor, adjoint):
    link_re = link_field[0]
    link_im = link_field[1]
    if adjoint:
        link_re = jnp.swapaxes(link_re, 0, 1)
        link_im = -jnp.swapaxes(link_im, 0, 1)
    spinor_re = spinor[:, 0][:, :, None]
    spinor_im = spinor[:, 1][:, :, None]
    out_re = lax.optimization_barrier(jnp.sum(link_re * spinor_re - link_im * spinor_im, axis=3))
    out_im = lax.optimization_barrier(jnp.sum(link_re * spinor_im + link_im * spinor_re, axis=3))
    return jnp.stack([out_re, out_im], axis=1)

def shifted(spinor, direction, offset):
    leading = spinor.shape[:-1]
    lattice = spinor.reshape(leading + (NY, LX))
    axis_index = [-1, -2, -3, -4][direction]
    rolled = jnp.roll(lattice, -offset, axis=axis_index)
    if direction == 3:
        boundary = NT - 1 if offset == 1 else 0
        factor = jnp.where(jnp.arange(NT) == boundary, -1.0, 1.0).astype(jnp.float32)
        rolled = rolled * factor[:, None, None, None]
    return rolled.reshape(spinor.shape)

def real_paths(weights):
    real_part = weights[:, :, :, 0]
    imag_part = weights[:, :, :, 1]
    blocks = jnp.stack([jnp.stack([real_part, -imag_part]), jnp.stack([imag_part, real_part])])
    return jnp.transpose(blocks, (2, 3, 0, 5, 4, 1, 6))

def dirac(spinor, gauge_links):
    minus_re, minus_im = projector_tables(-1.0)
    plus_re, plus_im = projector_tables(1.0)
    total = jnp.zeros_like(spinor)
    for direction in range(4):
        link_field = gauge_links[direction]
        upper_values = color_apply(link_field, shifted(spinor, direction, 1), False)
        lower_values = shifted(color_apply(link_field, spinor, True), direction, -1)
        total = total + spin_apply(minus_re[direction], minus_im[direction], upper_values)
        total = total + spin_apply(plus_re[direction], plus_im[direction], lower_values)
    return (4.0 + BARE_MASS) * spinor - 0.5 * total

def layer(weights, spinor, gauge_links):
    path_count = weights.shape[0]
    out_count = weights.shape[1]
    in_count = weights.shape[2]
    blocks = real_paths(weights).reshape(path_count, out_count * 8, in_count * 8)
    flat = spinor.reshape(in_count * 8, -1)

    def mixed(path):
        product = jnp.dot(blocks[path], flat, precision=HIGHEST_PRECISION, preferred_element_type=jnp.float32)
        return product.reshape((out_count,) + spinor.shape[1:])
    total = mixed(0)
    for direction in range(4):
        link_field = gauge_links[direction]
        total = total + color_apply(link_field, shifted(mixed(1 + 2 * direction), direction, 1), False)
        total = total + shifted(color_apply(link_field, mixed(2 + 2 * direction), True), direction, -1)
    return total

def restrict(near_null, mismatch):

    def one_vector(vector):
        vector = vector.astype(jnp.float32)
        real_part = lax.optimization_barrier(jnp.sum(vector[0] * mismatch[0] + vector[1] * mismatch[1], axis=(0, 1)))
        imag_part = lax.optimization_barrier(jnp.sum(vector[0] * mismatch[1] - vector[1] * mismatch[0], axis=(0, 1)))
        both = jnp.stack([real_part, imag_part]).reshape(2, NT // BLK, BLK, NZ // BLK, BLK, NY // BLK, BLK, LX // BLK, BLK)
        summed = lax.optimization_barrier(jnp.sum(both, axis=(2, 4, 6, 8)))
        return summed.reshape(2, NT // BLK, NZ // BLK, NY // BLK * (LX // BLK))
    coarse = lax.map(one_vector, near_null)
    return jnp.transpose(coarse, (1, 0, 2, 3, 4))

def reference(source, gauge_links, near_null, w_first, w_second):
    spinor = source[None]
    residual = dirac(spinor, gauge_links)

    def objective(first_weights, second_weights):
        hidden = layer(first_weights, residual, gauge_links)
        output = layer(second_weights, hidden, gauge_links)
        mismatch = output[0] - source
        coarse = restrict(near_null, mismatch)
        objective_value = (jnp.sum(mismatch * mismatch) + jnp.sum(coarse * coarse)) / (NT * NZ * NYX)
        return (objective_value, (output[0], coarse))
    gradients, outputs = jax.grad(objective, argnums=(0, 1), has_aux=True)(w_first, w_second)
    return (outputs[0], outputs[1], gradients[0], gradients[1])
```

```python
import functools

import jax
import jax.numpy as jnp
import numpy as np
from jax import lax
from jax.experimental import pallas as pl
from jax.experimental.pallas import tpu as pltpu
from jax.sharding import PartitionSpec as P

BLK = 4
NNULL = 24
LT = 4
LZ = 4
LX = 32
LANES = 128
ROWS = LT * LZ
WIDE = LZ * 3 * LANES
STACK = 80
BARE_MASS = -0.5
MESH = pl.DeviceIdType.MESH
F32 = jnp.float32
BF16 = jnp.bfloat16


def dirac_matrix():
    paulis = [
        np.array([[0, 1], [1, 0]], dtype=complex),
        np.array([[0, -1j], [1j, 0]], dtype=complex),
        np.array([[1, 0], [0, -1]], dtype=complex),
    ]
    corners = [-1j * matrix for matrix in paulis] + [np.eye(2, dtype=complex)]
    terms = [(4.0 + BARE_MASS) * np.eye(4)]
    for corner in corners:
        gamma = np.zeros((4, 4), dtype=complex)
        gamma[:2, 2:] = corner
        gamma[2:, :2] = corner.conj().T
        terms.append(-0.5 * (np.eye(4) - gamma))
        terms.append(-0.5 * (np.eye(4) + gamma))
    whole = np.zeros((16, STACK), dtype=np.float32)
    for path, term in enumerate(terms):
        block = np.block([[term.real, -term.imag], [term.imag, term.real]])
        whole[:8, path * 8 : path * 8 + 8] = block
    return np.concatenate([whole, whole], axis=1)


def whole_matrix(weights):
    real_part = weights[:, :, :, 0]
    imag_part = weights[:, :, :, 1]
    blocks = jnp.stack([jnp.stack([real_part, -imag_part]), jnp.stack([imag_part, real_part])])
    arranged = jnp.transpose(blocks, (3, 0, 5, 2, 4, 1, 6))
    return arranged.reshape(weights.shape[1] * 8, weights.shape[0], weights.shape[2] * 8)


def split_left(matrix):
    high = lax.reduce_precision(matrix, 8, 7)
    low = matrix - high
    both = jnp.concatenate([high, low], axis=0)
    return jnp.concatenate([both, both], axis=1).astype(BF16)


def kernel(
    sizes,
    source_ref,
    links_ref,
    null_hbm,
    dirac_ref,
    first_ref,
    second_ref,
    back_ref,
    out_ref,
    coarse_ref,
    grad_ref,
    null_ref,
    et,
    ez,
    dt,
    dz,
    ys,
    yr,
    dy,
    field,
    stack,
    x_first,
    hid,
    mixed,
    total,
    miss,
    cot,
    sums,
    spread_ref,
    red_y,
    red_z,
    red_t,
    send_sem,
    recv_sem,
    red_send,
    red_recv,
    null_sem,
):
    nt, nz, ny = sizes
    it = lax.axis_index("ta")
    iz = lax.axis_index("gz")
    iy = lax.axis_index("gy")
    null_copy = pltpu.make_async_copy(null_hbm, null_ref, null_sem)
    null_copy.start()

    barrier = pltpu.get_barrier_semaphore()
    for axis, mine, count in (("gy", iy, ny), ("gz", iz, nz), ("ta", it, nt)):
        for step in range(1, count):
            pl.semaphore_signal(
                barrier,
                inc=1,
                device_id={axis: lax.rem(mine + step, count)},
                device_id_type=MESH,
            )
    pl.semaphore_wait(barrier, nt + nz + ny - 3)

    row_id = lax.broadcasted_iota(jnp.int32, (8, LANES), 0)
    lane = lax.broadcasted_iota(jnp.int32, (8, LANES), 1)
    column = lane % LX
    sign = jnp.where(row_id < 4, -1.0, 1.0).astype(F32)
    wrap = it == nt - 1

    def link(mu, t, z):
        row = t * LZ + z

        def part(which, a, b):
            base = ((mu * 2 + which) * 9 + a * 3 + b) * ROWS
            return jnp.broadcast_to(links_ref[pl.ds(base + row, 1), :], (8, LANES))

        return part

    def turned(values):
        return [pltpu.roll(v, 4, 0) * sign for v in values]

    def time_sign(mu, t, values):
        if mu != 3:
            return values
        factor = jnp.where(jnp.logical_and(wrap, t == LT - 1), -1.0, 1.0).astype(F32)
        return [v * factor for v in values]

    def forward(mu, t, z, values):
        values = time_sign(mu, t, values)
        part = link(mu, t, z)
        spun = turned(values)
        outs = []
        for a in range(3):
            acc = None
            for b in range(3):
                term = part(0, a, b) * values[b] + part(1, a, b) * spun[b]
                acc = term if acc is None else acc + term
            outs.append(acc)
        return outs

    def adjoint(mu, t, z, values):
        values = time_sign(mu, t, values)
        part = link(mu, t, z)
        spun = turned(values)
        outs = []
        for a in range(3):
            acc = None
            for b in range(3):
                term = part(0, b, a) * values[b] - part(1, b, a) * spun[b]
                acc = term if acc is None else acc + term
            outs.append(acc)
        return outs

    def over_time(body, count=LT):
        def step(t, carry):
            body(t)
            return carry

        lax.fori_loop(0, count, step, 0)

    def exchange(rd, src_up, src_dn, put):
        def send(which, src, dst, axis, target):
            copy = pltpu.make_async_remote_copy(
                src_ref=src,
                dst_ref=dst,
                send_sem=send_sem.at[rd, which],
                recv_sem=recv_sem.at[rd, which],
                device_id={axis: target},
                device_id_type=MESH,
            )
            copy.start()
            return copy

        def y_part(t):
            ups, downs = [], []
            for z in range(LZ):
                up = src_up(1, t, z)
                down = adjoint(1, t, z, src_dn(1, t, z))
                for c in range(3):
                    dy[t, z, c] = down[c]
                ups.append(up)
                downs.append(down)

            def pack(f0, f1, d1, d0):
                left = jnp.where(lane < 32, f0, pltpu.roll(f1, 32, 1))
                right = jnp.where(lane < 96, pltpu.roll(d1, 96, 1), d0)
                return jnp.where(lane < 64, left, right)

            for z in range(LZ):
                ys[rd, t, z] = pack(ups[z][0], ups[z][1], downs[z][1], downs[z][0])
            for h in range(2):
                ys[rd, t, 4 + h] = pack(
                    ups[2 * h][2], ups[2 * h + 1][2], downs[2 * h + 1][2], downs[2 * h][2]
                )

        over_time(y_part)
        other = lax.rem(iy + 1, ny)
        c_y = send(0, ys.at[rd], yr.at[rd], "gy", other)

        def face_part(t):
            for z in range(LZ):
                up_t = src_up(3, t, z)
                up_z = src_up(2, t, z)
                for c in range(3):
                    et[rd, t, z, c] = up_t[c]
                    ez[rd, z, t, c] = up_z[c]

        over_time(face_part)
        c_tu = send(1, et.at[rd, 0], et.at[rd, LT], "ta", lax.rem(it + nt - 1, nt))
        c_zu = send(2, ez.at[rd, 0], ez.at[rd, LZ], "gz", lax.rem(iz + nz - 1, nz))

        def carry_t(t):
            for z in range(LZ):
                down = adjoint(3, t, z, src_dn(3, t, z))
                for c in range(3):
                    dt[rd, t + 1, z, c] = down[c]

        def carry_z(t, zs):
            for z in zs:
                down = adjoint(2, t, z, src_dn(2, t, z))
                for c in range(3):
                    dz[rd, z + 1, t, c] = down[c]

        carry_t(LT - 1)
        c_td = send(3, dt.at[rd, LT], dt.at[rd, 0], "ta", lax.rem(it + 1, nt))
        over_time(lambda t: carry_z(t, (LZ - 1,)))
        c_zd = send(4, dz.at[rd, LZ], dz.at[rd, 0], "gz", lax.rem(iz + 1, nz))

        over_time(carry_t, LT - 1)
        over_time(lambda t: carry_z(t, range(LZ - 1)))

        def x_part(t):
            for z in range(LZ):
                up = [
                    jnp.where(column == LX - 1, pltpu.roll(v, LX - 1, 1), pltpu.roll(v, LANES - 1, 1))
                    for v in src_up(0, t, z)
                ]
                put(1, t, z, forward(0, t, z, up))
                down = [
                    jnp.where(column == 0, pltpu.roll(v, LANES + 1 - LX, 1), pltpu.roll(v, 1, 1))
                    for v in adjoint(0, t, z, src_dn(0, t, z))
                ]
                put(2, t, z, down)

        over_time(x_part)
        c_tu.wait()
        c_td.wait()

        def t_part(t):
            for z in range(LZ):
                put(7, t, z, forward(3, t, z, [et[rd, t + 1, z, c] for c in range(3)]))
                put(8, t, z, [dt[rd, t, z, c] for c in range(3)])

        over_time(t_part)
        c_zu.wait()
        c_zd.wait()

        def z_part(t):
            for z in range(LZ):
                put(5, t, z, forward(2, t, z, [ez[rd, z + 1, t, c] for c in range(3)]))
                put(6, t, z, [dz[rd, z, t, c] for c in range(3)])

        over_time(z_part)
        c_y.wait()

        def y_take(t):
            for z in range(LZ):
                first = yr[rd, t, z]
                third = yr[rd, t, 4 + z // 2]
                f0, d0 = first, first
                f1, d1 = pltpu.roll(first, 96, 1), pltpu.roll(first, 32, 1)
                if z % 2 == 0:
                    f2, d2 = third, third
                else:
                    f2, d2 = pltpu.roll(third, 96, 1), pltpu.roll(third, 32, 1)
                up = src_up(1, t, z)
                up = [
                    pltpu.roll(jnp.where(lane < 32, halo, v), 96, 1)
                    for halo, v in zip((f0, f1, f2), up)
                ]
                put(3, t, z, forward(1, t, z, up))
                down = [
                    pltpu.roll(jnp.where(lane >= 96, halo, dy[t, z, c]), 32, 1)
                    for c, halo in enumerate((d0, d1, d2))
                ]
                put(4, t, z, down)

        over_time(y_take)

    def from_field(mu, t, z):
        return [field[t, z, c] for c in range(3)]

    def put_stack(path, t, z, values):
        for c in range(3):
            stack[t, z, c, path * 8 : path * 8 + 8, :] = values[c]

    def put_swapped(path, t, z, values):
        put_stack(path + 1 if path % 2 == 1 else path - 1, t, z, values)

    def split(values):
        high = values.astype(BF16)
        low = (values - high.astype(F32)).astype(BF16)
        return jnp.concatenate([high, low], axis=0)

    def identity_path():
        def step(t):
            for z in range(LZ):
                for c in range(3):
                    stack[t, z, c, 0:8, :] = field[t, z, c]

        over_time(step)

    def stacked_columns(t):
        return jnp.concatenate(
            [split(stack[t, z, c]) for z in range(LZ) for c in range(3)], axis=1
        )

    def dot(left, right):
        return lax.dot_general(
            left, right, (((1,), (0,)), ((), ())), preferred_element_type=F32
        )

    def dot_t(left, right):
        return lax.dot_general(
            left, right, (((1,), (1,)), ((), ())), preferred_element_type=F32
        )

    def load_source(ref):
        def step(t):
            for z in range(LZ):
                for c in range(3):
                    field[t, z, c] = ref[pl.ds(c * ROWS + t * LZ + z, 8, stride=3 * ROWS), :]

        over_time(step)

    def clear(t):
        for z in range(LZ):
            for c in range(3):
                stack[t, z, c, 72:80, :] = jnp.zeros((8, LANES), F32)

    over_time(clear)

    load_source(source_ref)
    identity_path()
    exchange(0, from_field, from_field, put_stack)

    def residual_step(t):
        result = dot(dirac_ref[...], stacked_columns(t))
        for z in range(LZ):
            for c in range(3):
                j = (z * 3 + c) * LANES
                field[t, z, c] = result[0:8, j : j + LANES]

    over_time(residual_step)

    identity_path()
    exchange(1, from_field, from_field, put_stack)

    def hidden_step(t):
        columns = stacked_columns(t)
        x_first[t] = columns
        result = dot(first_ref[...], columns)
        hid[t] = split(result[0:16] + result[16:32])
        product = dot(second_ref[...], hid[t])
        product = product[0:STACK] + product[STACK : 2 * STACK]
        for z in range(LZ):
            for c in range(3):
                j = (z * 3 + c) * LANES
                mixed[t, z, c] = product[:, j : j + LANES]
                total[t, z, c] = product[0:8, j : j + LANES]

    over_time(hidden_step)

    def mixed_up(mu, t, z):
        k = (1 + 2 * mu) * 8
        return [mixed[t, z, c, k : k + 8, :] for c in range(3)]

    def mixed_dn(mu, t, z):
        k = (2 + 2 * mu) * 8
        return [mixed[t, z, c, k : k + 8, :] for c in range(3)]

    def put_total(path, t, z, values):
        for c in range(3):
            total[t, z, c] += values[c]

    exchange(2, mixed_up, mixed_dn, put_total)

    def store_out(t):
        for z in range(LZ):
            for c in range(3):
                out_ref[pl.ds(c * ROWS + t * LZ + z, 8, stride=3 * ROWS), :] = total[t, z, c]

    over_time(store_out)
    miss[...] = out_ref[...] - source_ref[...]
    null_copy.wait()

    def restrict_step(k, carry):
        re = jnp.zeros((ROWS, LANES), F32)
        im = jnp.zeros((ROWS, LANES), F32)
        for j in range(12):
            v_re = null_ref[pl.ds(pl.multiple_of((k * 24 + j) * ROWS, ROWS), ROWS), :].astype(F32)
            v_im = null_ref[
                pl.ds(pl.multiple_of((k * 24 + 12 + j) * ROWS, ROWS), ROWS), :
            ].astype(F32)
            m_re = miss[j * ROWS : (j + 1) * ROWS, :]
            m_im = miss[(12 + j) * ROWS : (13 + j) * ROWS, :]
            re = re + (v_re * m_re + v_im * m_im)
            im = im + (v_re * m_im - v_im * m_re)
        sums[pl.ds(k, 1), :] = jnp.sum(re, axis=0, keepdims=True)
        sums[pl.ds(NNULL + k, 1), :] = jnp.sum(im, axis=0, keepdims=True)
        return carry

    lax.fori_loop(0, NNULL, restrict_step, 0)
    left = lax.broadcasted_iota(jnp.int32, (LANES, LANES), 0) % LX // BLK
    right = lax.broadcasted_iota(jnp.int32, (LANES, LANES), 1)
    highest = lax.Precision.HIGHEST
    flat = sums[...]
    same = (left == right % LX // BLK).astype(F32)
    pick = (left == right).astype(F32)
    spread_ref[...] = jnp.dot(flat, same, precision=highest, preferred_element_type=F32)
    coarse_ref[...] = jnp.dot(flat, pick, precision=highest, preferred_element_type=F32)

    scale = 2.0 / (ROWS * LANES * nt * nz * ny)

    def prolong_step(j, carry):
        re = miss[pl.ds(pl.multiple_of(j * ROWS, ROWS), ROWS), :]
        im = miss[pl.ds(pl.multiple_of((12 + j) * ROWS, ROWS), ROWS), :]
        for k in range(NNULL):
            v_re = null_ref[pl.ds(pl.multiple_of((k * 24 + j) * ROWS, ROWS), ROWS), :].astype(F32)
            v_im = null_ref[
                pl.ds(pl.multiple_of((k * 24 + 12 + j) * ROWS, ROWS), ROWS), :
            ].astype(F32)
            s_re = spread_ref[k : k + 1, :]
            s_im = spread_ref[NNULL + k : NNULL + k + 1, :]
            re = re + (s_re * v_re - s_im * v_im)
            im = im + (s_re * v_im + s_im * v_re)
        cot[pl.ds(pl.multiple_of(j * ROWS, ROWS), ROWS), :] = re * scale
        cot[pl.ds(pl.multiple_of((12 + j) * ROWS, ROWS), ROWS), :] = im * scale
        return carry

    lax.fori_loop(0, 12, prolong_step, 0)

    load_source(cot)
    identity_path()
    exchange(3, from_field, from_field, put_swapped)

    def back_step(t, carry):
        first_sum, second_sum = carry
        columns = stacked_columns(t)
        result = dot(back_ref[...], columns)
        back = split(result[0:16] + result[16:32])
        first_cols = x_first[t]
        g1 = dot_t(back, first_cols[0:STACK]) + dot_t(back, first_cols[STACK : 2 * STACK])
        g2 = dot_t(hid[t], columns[0:STACK]) + dot_t(hid[t], columns[STACK : 2 * STACK])
        return first_sum + g1[0:16] + g1[16:32], second_sum + g2[0:16] + g2[16:32]

    zero = jnp.zeros((16, STACK), F32)
    first_sum, second_sum = lax.fori_loop(0, LT, back_step, (zero, zero))

    grad_ref[...] = jnp.zeros_like(grad_ref)
    grad_ref[0:16, 0:STACK] = first_sum
    grad_ref[16:32, 0:STACK] = second_sum
    base = 0
    for axis, mine, count, slots in (
        ("gy", iy, ny, red_y),
        ("gz", iz, nz, red_z),
        ("ta", it, nt, red_t),
    ):
        slots[mine] = grad_ref[...]
        copies = []
        for step in range(1, count):
            copy = pltpu.make_async_remote_copy(
                src_ref=slots.at[mine],
                dst_ref=slots.at[mine],
                send_sem=red_send.at[base + step],
                recv_sem=red_recv.at[base + step],
                device_id={axis: lax.rem(mine + step, count)},
                device_id_type=MESH,
            )
            copy.start()
            copies.append(copy)
        for copy in copies:
            copy.wait()
        acc = slots[0]
        for j in range(1, count):
            acc = acc + slots[j]
        grad_ref[...] = acc
        base += count


def body(sizes, source, gauge_links, near_null, w_first, w_second):
    nt, nz, ny = sizes
    first = whole_matrix(w_first).reshape(16, 72)
    second = jnp.transpose(whole_matrix(w_second), (1, 0, 2)).reshape(72, 16)
    first_left = split_left(jnp.pad(first, ((0, 0), (0, 8))))
    second_pad = jnp.pad(second, ((0, 8), (0, 0)))
    second_left = split_left(second_pad)
    back_left = split_left(second_pad.T)
    vmem = pl.BlockSpec(memory_space=pltpu.VMEM)
    slab = (3, 8, LANES)
    out, coarse, grad = pl.pallas_call(
        functools.partial(kernel, sizes),
        out_shape=(
            jax.ShapeDtypeStruct((24 * ROWS, LANES), F32),
            jax.ShapeDtypeStruct((2 * NNULL, LANES), F32),
            jax.ShapeDtypeStruct((32, LANES), F32),
        ),
        in_specs=[vmem, vmem, pl.BlockSpec(memory_space=pl.ANY), vmem, vmem, vmem, vmem],
        out_specs=(vmem, vmem, vmem),
        scratch_shapes=[
            pltpu.VMEM((NNULL * 24 * ROWS, LANES), BF16),
            pltpu.VMEM((4, LT + 1, LZ) + slab, F32),
            pltpu.VMEM((4, LZ + 1, LT) + slab, F32),
            pltpu.VMEM((4, LT + 1, LZ) + slab, F32),
            pltpu.VMEM((4, LZ + 1, LT) + slab, F32),
            pltpu.VMEM((4, LT, 6, 8, LANES), F32),
            pltpu.VMEM((4, LT, 6, 8, LANES), F32),
            pltpu.VMEM((LT, LZ) + slab, F32),
            pltpu.VMEM((LT, LZ) + slab, F32),
            pltpu.VMEM((LT, LZ, 3, STACK, LANES), F32),
            pltpu.VMEM((LT, 2 * STACK, WIDE), BF16),
            pltpu.VMEM((LT, 32, WIDE), BF16),
            pltpu.VMEM((LT, LZ, 3, STACK, LANES), F32),
            pltpu.VMEM((LT, LZ) + slab, F32),
            pltpu.VMEM((24 * ROWS, LANES), F32),
            pltpu.VMEM((24 * ROWS, LANES), F32),
            pltpu.VMEM((2 * NNULL, LANES), F32),
            pltpu.VMEM((2 * NNULL, LANES), F32),
            pltpu.VMEM((ny, 32, LANES), F32),
            pltpu.VMEM((nz, 32, LANES), F32),
            pltpu.VMEM((nt, 32, LANES), F32),
            pltpu.SemaphoreType.DMA((4, 5)),
            pltpu.SemaphoreType.DMA((4, 5)),
            pltpu.SemaphoreType.DMA((nt + nz + ny,)),
            pltpu.SemaphoreType.DMA((nt + nz + ny,)),
            pltpu.SemaphoreType.DMA,
        ],
        compiler_params=pltpu.CompilerParams(
            collective_id=0, has_side_effects=True, vmem_limit_bytes=48 * 1024 * 1024
        ),
    )(
        source.reshape(24 * ROWS, LANES),
        gauge_links.reshape(72 * ROWS, LANES),
        near_null.reshape(NNULL * 24 * ROWS, LANES),
        jnp.asarray(dirac_matrix(), BF16),
        first_left,
        second_left,
        back_left,
    )

    one = grad[0:16, 0:72].reshape(2, 2, 4, 9, 1, 2, 4)
    two = jnp.transpose(grad[16:32, 0:72].reshape(2, 2, 4, 9, 2, 4, 1), (6, 4, 5, 3, 0, 1, 2))

    def merge(product):
        real_grad = product[:, 0, :, :, :, 0] + product[:, 1, :, :, :, 1]
        imag_grad = product[:, 1, :, :, :, 0] - product[:, 0, :, :, :, 1]
        return jnp.transpose(jnp.stack([real_grad, imag_grad]), (3, 1, 4, 0, 2, 5))

    return (
        out.reshape(source.shape),
        coarse[:, : LX // BLK].reshape(2, NNULL, 1, 1, LX // BLK),
        merge(one),
        merge(two),
    )


def solution(mesh):
    sizes = (mesh.shape["ta"], mesh.shape["gz"], mesh.shape["gy"])
    in_specs = (
        P(None, None, None, "ta", "gz", "gy"),
        P(None, None, None, None, "ta", "gz", "gy"),
        P(None, None, None, None, "ta", "gz", "gy"),
        P(),
        P(),
    )
    out_specs = (P(None, None, None, "ta", "gz", "gy"), P(None, None, "ta", "gz", "gy"), P(), P())
    return jax.shard_map(
        functools.partial(body, sizes),
        mesh=mesh,
        in_specs=in_specs,
        out_specs=out_specs,
        check_vma=False,
    )
```

```python
import functools

import jax
import jax.numpy as jnp
import numpy as np
from jax import lax
from jax.experimental import pallas as pl
from jax.experimental.pallas import tpu as pltpu
from jax.sharding import PartitionSpec as P

BLK = 4
NNULL = 24
LT = 4
LZ = 4
LX = 32
LANES = 128
ROWS = LT * LZ
WIDE = LZ * 3 * LANES
STACK = 80
BARE_MASS = -0.5
MESH = pl.DeviceIdType.MESH
F32 = jnp.float32
BF16 = jnp.bfloat16


def dirac_matrix():
    paulis = [
        np.array([[0, 1], [1, 0]], dtype=complex),
        np.array([[0, -1j], [1j, 0]], dtype=complex),
        np.array([[1, 0], [0, -1]], dtype=complex),
    ]
    corners = [-1j * matrix for matrix in paulis] + [np.eye(2, dtype=complex)]
    terms = [(4.0 + BARE_MASS) * np.eye(4)]
    for corner in corners:
        gamma = np.zeros((4, 4), dtype=complex)
        gamma[:2, 2:] = corner
        gamma[2:, :2] = corner.conj().T
        terms.append(-0.5 * (np.eye(4) - gamma))
        terms.append(-0.5 * (np.eye(4) + gamma))
    whole = np.zeros((16, STACK), dtype=np.float32)
    for path, term in enumerate(terms):
        block = np.block([[term.real, -term.imag], [term.imag, term.real]])
        whole[:8, path * 8 : path * 8 + 8] = block
    return np.concatenate([whole, whole], axis=1)


def index_maps(width):
    row = lax.broadcasted_iota(jnp.int32, (128, width), 0)
    col = lax.broadcasted_iota(jnp.int32, (128, width), 1)
    mask = jnp.where(row < 64, row % 4, row // 4 % 4) == col % 4
    return mask, col // 4 % 2


def left_maps(shape, row_dim, mat_dim):
    row = lax.broadcasted_iota(jnp.int32, shape, row_dim)
    mat = lax.broadcasted_iota(jnp.int32, shape, mat_dim)
    first = row < 64
    part, part_mat = row // 16 % 2, mat // 4 % 2
    match = jnp.logical_and(row // 32 == mat // 8, jnp.where(first, row // 4 % 4, row % 4) == mat % 4)
    same = part == part_mat
    sign_same = jnp.where(jnp.logical_or(first, part_mat == 0), 1.0, -1.0)
    sign_cross = jnp.where(jnp.logical_and(first, part_mat == 0), -1.0, 1.0)
    keep = jnp.where(jnp.logical_and(match, same), sign_same, 0.0).astype(F32)
    swap = jnp.where(jnp.logical_and(match, jnp.logical_not(same)), sign_cross, 0.0).astype(F32)
    return keep, swap


def exact_dot(left, right):
    return jnp.dot(left, right, precision=lax.Precision.HIGHEST, preferred_element_type=F32)


def spread_weights(values):
    width = 2 * STACK
    row = lax.broadcasted_iota(jnp.int32, (9, width), 0)
    col = lax.broadcasted_iota(jnp.int32, (9, width), 1)
    path = (row == jnp.where(col >= STACK, col - STACK, col) // 8).astype(F32)
    wide = exact_dot(values, path)
    mask, kind = index_maps(width)
    keep, swap = left_maps((32, 128), 1, 0)
    wide = jnp.where(mask, wide, 0.0)
    straight = jnp.where(kind == 0, wide, 0.0)
    return exact_dot(keep, straight) + exact_dot(swap, wide - straight)


def gather_weights(product):
    keep, swap = left_maps((128, 32), 0, 1)
    mask, kind = index_maps(STACK)
    wide = jnp.where(kind == 0, exact_dot(keep, product), exact_dot(swap, product))
    wide = jnp.where(mask, wide, 0.0)
    row = lax.broadcasted_iota(jnp.int32, (STACK, 9), 0)
    col = lax.broadcasted_iota(jnp.int32, (STACK, 9), 1)
    return exact_dot(wide, (row // 8 == col).astype(F32))


def kernel(
    sizes,
    source_hbm,
    links_hbm,
    null_hbm,
    w_first_hbm,
    w_second_hbm,
    dirac_hbm,
    out_ref,
    coarse_ref,
    weight_ref,
    source_ref,
    links_ref,
    null_ref,
    w_ref,
    dirac_ref,
    first_ref,
    second_ref,
    back_ref,
    grad_ref,
    et,
    ez,
    dt,
    dz,
    ys,
    yr,
    dy,
    field,
    stack,
    x_first,
    hid,
    mixed,
    total,
    miss,
    cot,
    sums,
    spread_ref,
    red_y,
    red_z,
    red_t,
    send_sem,
    recv_sem,
    red_send,
    red_recv,
    load_sem,
):
    nt, nz, ny = sizes
    it = lax.axis_index("ta")
    iz = lax.axis_index("gz")
    iy = lax.axis_index("gy")
    link_rows = 18 * ROWS

    def link_slice(ref, mu):
        return ref.at[pl.ds(mu * link_rows, link_rows), :]

    loads = [
        (source_hbm, source_ref),
        (link_slice(links_hbm, 1), link_slice(links_ref, 1)),
        (link_slice(links_hbm, 3), link_slice(links_ref, 3)),
        (link_slice(links_hbm, 2), link_slice(links_ref, 2)),
        (link_slice(links_hbm, 0), link_slice(links_ref, 0)),
        (dirac_hbm, dirac_ref),
        (w_first_hbm, w_ref.at[0]),
        (w_second_hbm, w_ref.at[1]),
        (null_hbm, null_ref),
    ]
    loads = [
        pltpu.make_async_copy(src, dst, load_sem.at[k]) for k, (src, dst) in enumerate(loads)
    ]
    for load in loads:
        load.start()
    null_copy = loads.pop()

    barrier = pltpu.get_barrier_semaphore()
    for axis, mine, count in (("gy", iy, ny), ("gz", iz, nz), ("ta", it, nt)):
        for step in range(1, count):
            pl.semaphore_signal(
                barrier,
                inc=1,
                device_id={axis: lax.rem(mine + step, count)},
                device_id_type=MESH,
            )
    pl.semaphore_wait(barrier, nt + nz + ny - 3)

    row_id = lax.broadcasted_iota(jnp.int32, (8, LANES), 0)
    lane = lax.broadcasted_iota(jnp.int32, (8, LANES), 1)
    column = lane % LX
    sign = jnp.where(row_id < 4, -1.0, 1.0).astype(F32)
    wrap = it == nt - 1

    def link(mu, t, z):
        row = t * LZ + z

        def part(which, a, b):
            base = ((mu * 2 + which) * 9 + a * 3 + b) * ROWS
            return jnp.broadcast_to(links_ref[pl.ds(base + row, 1), :], (8, LANES))

        return part

    def turned(values):
        return [pltpu.roll(v, 4, 0) * sign for v in values]

    def time_sign(mu, t, values):
        if mu != 3:
            return values
        factor = jnp.where(jnp.logical_and(wrap, t == LT - 1), -1.0, 1.0).astype(F32)
        return [v * factor for v in values]

    def forward(mu, t, z, values):
        values = time_sign(mu, t, values)
        part = link(mu, t, z)
        spun = turned(values)
        outs = []
        for a in range(3):
            acc = None
            for b in range(3):
                term = part(0, a, b) * values[b] + part(1, a, b) * spun[b]
                acc = term if acc is None else acc + term
            outs.append(acc)
        return outs

    def adjoint(mu, t, z, values):
        values = time_sign(mu, t, values)
        part = link(mu, t, z)
        spun = turned(values)
        outs = []
        for a in range(3):
            acc = None
            for b in range(3):
                term = part(0, b, a) * values[b] - part(1, b, a) * spun[b]
                acc = term if acc is None else acc + term
            outs.append(acc)
        return outs

    def over_time(body, count=LT):
        def step(t, carry):
            body(t)
            return carry

        lax.fori_loop(0, count, step, 0)

    def exchange(rd, src_up, src_dn, put, meanwhile=None):
        def send(which, src, dst, axis, target):
            copy = pltpu.make_async_remote_copy(
                src_ref=src,
                dst_ref=dst,
                send_sem=send_sem.at[rd, which],
                recv_sem=recv_sem.at[rd, which],
                device_id={axis: target},
                device_id_type=MESH,
            )
            copy.start()
            return copy

        def y_part(t):
            ups, downs = [], []
            for z in range(LZ):
                up = src_up(1, t, z)
                down = adjoint(1, t, z, src_dn(1, t, z))
                for c in range(3):
                    dy[t, z, c] = down[c]
                ups.append(up)
                downs.append(down)

            def pack(f0, f1, d1, d0):
                left = jnp.where(lane < 32, f0, pltpu.roll(f1, 32, 1))
                right = jnp.where(lane < 96, pltpu.roll(d1, 96, 1), d0)
                return jnp.where(lane < 64, left, right)

            for z in range(LZ):
                ys[rd, t, z] = pack(ups[z][0], ups[z][1], downs[z][1], downs[z][0])
            for h in range(2):
                ys[rd, t, 4 + h] = pack(
                    ups[2 * h][2], ups[2 * h + 1][2], downs[2 * h + 1][2], downs[2 * h][2]
                )

        over_time(y_part)
        other = lax.rem(iy + 1, ny)
        c_y = send(0, ys.at[rd], yr.at[rd], "gy", other)

        def face_part(t):
            for z in range(LZ):
                up_t = src_up(3, t, z)
                up_z = src_up(2, t, z)
                for c in range(3):
                    et[rd, t, z, c] = up_t[c]
                    ez[rd, z, t, c] = up_z[c]

        over_time(face_part)
        c_tu = send(1, et.at[rd, 0], et.at[rd, LT], "ta", lax.rem(it + nt - 1, nt))
        c_zu = send(2, ez.at[rd, 0], ez.at[rd, LZ], "gz", lax.rem(iz + nz - 1, nz))

        def carry_t(t):
            for z in range(LZ):
                down = adjoint(3, t, z, src_dn(3, t, z))
                for c in range(3):
                    dt[rd, t + 1, z, c] = down[c]

        def carry_z(t, zs):
            for z in zs:
                down = adjoint(2, t, z, src_dn(2, t, z))
                for c in range(3):
                    dz[rd, z + 1, t, c] = down[c]

        carry_t(LT - 1)
        c_td = send(3, dt.at[rd, LT], dt.at[rd, 0], "ta", lax.rem(it + 1, nt))
        over_time(lambda t: carry_z(t, (LZ - 1,)))
        c_zd = send(4, dz.at[rd, LZ], dz.at[rd, 0], "gz", lax.rem(iz + 1, nz))

        over_time(carry_t, LT - 1)
        over_time(lambda t: carry_z(t, range(LZ - 1)))

        def x_part(t):
            for z in range(LZ):
                up = [
                    jnp.where(column == LX - 1, pltpu.roll(v, LX - 1, 1), pltpu.roll(v, LANES - 1, 1))
                    for v in src_up(0, t, z)
                ]
                put(1, t, z, forward(0, t, z, up))
                down = [
                    jnp.where(column == 0, pltpu.roll(v, LANES + 1 - LX, 1), pltpu.roll(v, 1, 1))
                    for v in adjoint(0, t, z, src_dn(0, t, z))
                ]
                put(2, t, z, down)

        over_time(x_part)
        if meanwhile is not None:
            meanwhile()
        c_tu.wait()
        c_td.wait()

        def t_part(t):
            for z in range(LZ):
                put(7, t, z, forward(3, t, z, [et[rd, t + 1, z, c] for c in range(3)]))
                put(8, t, z, [dt[rd, t, z, c] for c in range(3)])

        over_time(t_part)
        c_zu.wait()
        c_zd.wait()

        def z_part(t):
            for z in range(LZ):
                put(5, t, z, forward(2, t, z, [ez[rd, z + 1, t, c] for c in range(3)]))
                put(6, t, z, [dz[rd, z, t, c] for c in range(3)])

        over_time(z_part)
        c_y.wait()

        def y_take(t):
            for z in range(LZ):
                first = yr[rd, t, z]
                third = yr[rd, t, 4 + z // 2]
                f0, d0 = first, first
                f1, d1 = pltpu.roll(first, 96, 1), pltpu.roll(first, 32, 1)
                if z % 2 == 0:
                    f2, d2 = third, third
                else:
                    f2, d2 = pltpu.roll(third, 96, 1), pltpu.roll(third, 32, 1)
                up = src_up(1, t, z)
                up = [
                    pltpu.roll(jnp.where(lane < 32, halo, v), 96, 1)
                    for halo, v in zip((f0, f1, f2), up)
                ]
                put(3, t, z, forward(1, t, z, up))
                down = [
                    pltpu.roll(jnp.where(lane >= 96, halo, dy[t, z, c]), 32, 1)
                    for c, halo in enumerate((d0, d1, d2))
                ]
                put(4, t, z, down)

        over_time(y_take)

    def from_field(mu, t, z):
        return [field[t, z, c] for c in range(3)]

    def put_stack(path, t, z, values):
        for c in range(3):
            stack[t, z, c, path * 8 : path * 8 + 8, :] = values[c]

    def put_swapped(path, t, z, values):
        put_stack(path + 1 if path % 2 == 1 else path - 1, t, z, values)

    def split(values):
        high = values.astype(BF16)
        low = (values - high.astype(F32)).astype(BF16)
        return jnp.concatenate([high, low], axis=0)

    def identity_path():
        def step(t):
            for z in range(LZ):
                for c in range(3):
                    stack[t, z, c, 0:8, :] = field[t, z, c]

        over_time(step)

    def stacked_columns(t):
        return jnp.concatenate(
            [split(stack[t, z, c]) for z in range(LZ) for c in range(3)], axis=1
        )

    def dot(left, right):
        return lax.dot_general(
            left, right, (((1,), (0,)), ((), ())), preferred_element_type=F32
        )

    def dot_t(left, right):
        return lax.dot_general(
            left, right, (((1,), (1,)), ((), ())), preferred_element_type=F32
        )

    def load_source(ref):
        def step(t):
            for z in range(LZ):
                for c in range(3):
                    field[t, z, c] = ref[pl.ds(c * ROWS + t * LZ + z, 8, stride=3 * ROWS), :]

        over_time(step)

    def clear(t):
        for z in range(LZ):
            for c in range(3):
                stack[t, z, c, 72:80, :] = jnp.zeros((8, LANES), F32)

    over_time(clear)

    def prepare():
        for load in loads[5:]:
            load.wait()
        values = spread_weights(w_ref[...].reshape(128, 9))
        high = values.astype(BF16)
        low = values - high.astype(F32)
        low = low.astype(BF16)
        first_ref[...] = jnp.concatenate([high[0:16], low[0:16]], axis=0)
        back_ref[...] = jnp.concatenate([high[16:32], low[16:32]], axis=0)
        col = lax.broadcasted_iota(jnp.int32, (16, 2 * STACK), 1)
        mixing = jnp.where(col < STACK, high[16:32].astype(F32), low[16:32].astype(F32))
        mixing = jnp.concatenate([mixing, mixing], axis=0)
        second_ref[...] = jnp.transpose(mixing).astype(BF16)

    loads[0].wait()
    load_source(source_ref)
    identity_path()
    for load in loads[1:5]:
        load.wait()
    exchange(0, from_field, from_field, put_stack, prepare)

    def residual_step(t):
        result = dot(dirac_ref[...].astype(BF16), stacked_columns(t))
        for z in range(LZ):
            for c in range(3):
                j = (z * 3 + c) * LANES
                field[t, z, c] = result[0:8, j : j + LANES]

    over_time(residual_step)

    identity_path()
    exchange(1, from_field, from_field, put_stack)

    def hidden_step(t):
        columns = stacked_columns(t)
        x_first[t] = columns
        result = dot(first_ref[...], columns)
        hid[t] = split(result[0:16] + result[16:32])
        product = dot(second_ref[...], hid[t])
        product = product[0:STACK] + product[STACK : 2 * STACK]
        for z in range(LZ):
            for c in range(3):
                j = (z * 3 + c) * LANES
                mixed[t, z, c] = product[:, j : j + LANES]
                total[t, z, c] = product[0:8, j : j + LANES]

    over_time(hidden_step)

    def mixed_up(mu, t, z):
        k = (1 + 2 * mu) * 8
        return [mixed[t, z, c, k : k + 8, :] for c in range(3)]

    def mixed_dn(mu, t, z):
        k = (2 + 2 * mu) * 8
        return [mixed[t, z, c, k : k + 8, :] for c in range(3)]

    def put_total(path, t, z, values):
        for c in range(3):
            total[t, z, c] += values[c]

    exchange(2, mixed_up, mixed_dn, put_total)

    def store_out(t):
        for z in range(LZ):
            for c in range(3):
                out_ref[pl.ds(c * ROWS + t * LZ + z, 8, stride=3 * ROWS), :] = total[t, z, c]

    over_time(store_out)
    miss[...] = out_ref[...] - source_ref[...]
    null_copy.wait()

    def restrict_step(k, carry):
        re = jnp.zeros((ROWS, LANES), F32)
        im = jnp.zeros((ROWS, LANES), F32)
        for j in range(12):
            v_re = null_ref[pl.ds(pl.multiple_of((k * 24 + j) * ROWS, ROWS), ROWS), :].astype(F32)
            v_im = null_ref[
                pl.ds(pl.multiple_of((k * 24 + 12 + j) * ROWS, ROWS), ROWS), :
            ].astype(F32)
            m_re = miss[j * ROWS : (j + 1) * ROWS, :]
            m_im = miss[(12 + j) * ROWS : (13 + j) * ROWS, :]
            re = re + (v_re * m_re + v_im * m_im)
            im = im + (v_re * m_im - v_im * m_re)
        sums[pl.ds(k, 1), :] = jnp.sum(re, axis=0, keepdims=True)
        sums[pl.ds(NNULL + k, 1), :] = jnp.sum(im, axis=0, keepdims=True)
        return carry

    lax.fori_loop(0, NNULL, restrict_step, 0)
    left = lax.broadcasted_iota(jnp.int32, (LANES, LANES), 0) % LX // BLK
    right = lax.broadcasted_iota(jnp.int32, (LANES, LANES), 1) % LX // BLK
    spread_ref[...] = exact_dot(sums[...], (left == right).astype(F32))
    block = lax.broadcasted_iota(jnp.int32, (8, LANES), 0)
    pick = (block == column // BLK).astype(F32)
    for half in range(2):
        coarse_ref[half * 8 : half * 8 + 8, :] = lax.dot_general(
            pick,
            sums[half * NNULL : (half + 1) * NNULL, :],
            (((1,), (1,)), ((), ())),
            precision=lax.Precision.HIGHEST,
            preferred_element_type=F32,
        )

    scale = 2.0 / (ROWS * LANES * nt * nz * ny)

    def prolong_step(j, carry):
        re = miss[pl.ds(pl.multiple_of(j * ROWS, ROWS), ROWS), :]
        im = miss[pl.ds(pl.multiple_of((12 + j) * ROWS, ROWS), ROWS), :]
        for k in range(NNULL):
            v_re = null_ref[pl.ds(pl.multiple_of((k * 24 + j) * ROWS, ROWS), ROWS), :].astype(F32)
            v_im = null_ref[
                pl.ds(pl.multiple_of((k * 24 + 12 + j) * ROWS, ROWS), ROWS), :
            ].astype(F32)
            s_re = spread_ref[k : k + 1, :]
            s_im = spread_ref[NNULL + k : NNULL + k + 1, :]
            re = re + (s_re * v_re - s_im * v_im)
            im = im + (s_re * v_im + s_im * v_re)
        cot[pl.ds(pl.multiple_of(j * ROWS, ROWS), ROWS), :] = re * scale
        cot[pl.ds(pl.multiple_of((12 + j) * ROWS, ROWS), ROWS), :] = im * scale
        return carry

    lax.fori_loop(0, 12, prolong_step, 0)

    load_source(cot)
    identity_path()
    exchange(3, from_field, from_field, put_swapped)

    def back_step(t, carry):
        first_sum, second_sum = carry
        columns = stacked_columns(t)
        result = dot(back_ref[...], columns)
        back = split(result[0:16] + result[16:32])
        first_cols = x_first[t]
        g1 = dot_t(back, first_cols[0:STACK]) + dot_t(back, first_cols[STACK : 2 * STACK])
        g2 = dot_t(hid[t], columns[0:STACK]) + dot_t(hid[t], columns[STACK : 2 * STACK])
        return first_sum + g1[0:16] + g1[16:32], second_sum + g2[0:16] + g2[16:32]

    zero = jnp.zeros((16, STACK), F32)
    first_sum, second_sum = lax.fori_loop(0, LT, back_step, (zero, zero))

    grad_ref[...] = jnp.zeros_like(grad_ref)
    grad_ref[0:16, 0:STACK] = first_sum
    grad_ref[16:32, 0:STACK] = second_sum
    base = 0
    for axis, mine, count, slots in (
        ("gy", iy, ny, red_y),
        ("gz", iz, nz, red_z),
        ("ta", it, nt, red_t),
    ):
        slots[mine] = grad_ref[...]
        copies = []
        for step in range(1, count):
            copy = pltpu.make_async_remote_copy(
                src_ref=slots.at[mine],
                dst_ref=slots.at[mine],
                send_sem=red_send.at[base + step],
                recv_sem=red_recv.at[base + step],
                device_id={axis: lax.rem(mine + step, count)},
                device_id_type=MESH,
            )
            copy.start()
            copies.append(copy)
        for copy in copies:
            copy.wait()
        acc = slots[0]
        for j in range(1, count):
            acc = acc + slots[j]
        grad_ref[...] = acc
        base += count
    weight_ref[...] = gather_weights(grad_ref[:, 0:STACK])


def store_kernel(out_ref, coarse_ref, weight_ref, out_hbm, coarse_hbm, first_hbm, second_hbm, sem):
    pairs = [
        (out_ref, out_hbm),
        (coarse_ref, coarse_hbm),
        (weight_ref.at[0:64, :], first_hbm),
        (weight_ref.at[64:128, :], second_hbm),
    ]
    copies = [pltpu.make_async_copy(src, dst, sem.at[k]) for k, (src, dst) in enumerate(pairs)]
    for copy in copies:
        copy.start()
    for copy in copies:
        copy.wait()


def body(sizes, source, gauge_links, near_null, w_first, w_second):
    nt, nz, ny = sizes
    vmem = pl.BlockSpec(memory_space=pltpu.VMEM)
    slab = (3, 8, LANES)
    hbm = pl.BlockSpec(memory_space=pltpu.HBM)
    out, coarse, grad = pl.pallas_call(
        functools.partial(kernel, sizes),
        out_shape=(
            jax.ShapeDtypeStruct((24 * ROWS, LANES), F32),
            jax.ShapeDtypeStruct((16, NNULL), F32),
            jax.ShapeDtypeStruct((128, 9), F32),
        ),
        in_specs=[hbm] * 6,
        out_specs=(vmem, vmem, vmem),
        scratch_shapes=[
            pltpu.VMEM((24 * ROWS, LANES), F32),
            pltpu.VMEM((72 * ROWS, LANES), F32),
            pltpu.VMEM((NNULL * 24 * ROWS, LANES), BF16),
            pltpu.VMEM((2, 64, 9), F32),
            pltpu.VMEM((16, 2 * STACK), F32),
            pltpu.VMEM((32, 2 * STACK), BF16),
            pltpu.VMEM((2 * STACK, 32), BF16),
            pltpu.VMEM((32, 2 * STACK), BF16),
            pltpu.VMEM((32, LANES), F32),
            pltpu.VMEM((4, LT + 1, LZ) + slab, F32),
            pltpu.VMEM((4, LZ + 1, LT) + slab, F32),
            pltpu.VMEM((4, LT + 1, LZ) + slab, F32),
            pltpu.VMEM((4, LZ + 1, LT) + slab, F32),
            pltpu.VMEM((4, LT, 6, 8, LANES), F32),
            pltpu.VMEM((4, LT, 6, 8, LANES), F32),
            pltpu.VMEM((LT, LZ) + slab, F32),
            pltpu.VMEM((LT, LZ) + slab, F32),
            pltpu.VMEM((LT, LZ, 3, STACK, LANES), F32),
            pltpu.VMEM((LT, 2 * STACK, WIDE), BF16),
            pltpu.VMEM((LT, 32, WIDE), BF16),
            pltpu.VMEM((LT, LZ, 3, STACK, LANES), F32),
            pltpu.VMEM((LT, LZ) + slab, F32),
            pltpu.VMEM((24 * ROWS, LANES), F32),
            pltpu.VMEM((24 * ROWS, LANES), F32),
            pltpu.VMEM((2 * NNULL, LANES), F32),
            pltpu.VMEM((2 * NNULL, LANES), F32),
            pltpu.VMEM((ny, 32, LANES), F32),
            pltpu.VMEM((nz, 32, LANES), F32),
            pltpu.VMEM((nt, 32, LANES), F32),
            pltpu.SemaphoreType.DMA((4, 5)),
            pltpu.SemaphoreType.DMA((4, 5)),
            pltpu.SemaphoreType.DMA((nt + nz + ny,)),
            pltpu.SemaphoreType.DMA((nt + nz + ny,)),
            pltpu.SemaphoreType.DMA((9,)),
        ],
        compiler_params=pltpu.CompilerParams(
            collective_id=0, has_side_effects=True, vmem_limit_bytes=(65536 - 288) * 1024
        ),
    )(
        source.reshape(24 * ROWS, LANES),
        gauge_links.reshape(72 * ROWS, LANES),
        near_null.reshape(NNULL * 24 * ROWS, LANES),
        jnp.transpose(w_first, (1, 2, 3, 4, 5, 0)).reshape(64, 9),
        jnp.transpose(w_second, (1, 2, 3, 4, 5, 0)).reshape(64, 9),
        jnp.asarray(dirac_matrix()),
    )
    out, coarse, first, second = pl.pallas_call(
        store_kernel,
        out_shape=(
            jax.ShapeDtypeStruct((24 * ROWS, LANES), F32),
            jax.ShapeDtypeStruct((16, NNULL), F32),
            jax.ShapeDtypeStruct((64, 9), F32),
            jax.ShapeDtypeStruct((64, 9), F32),
        ),
        in_specs=[vmem] * 3,
        out_specs=(hbm,) * 4,
        scratch_shapes=[pltpu.SemaphoreType.DMA((4,))],
    )(out, coarse, grad)

    def as_weights(values, outs, ins):
        return jnp.transpose(values.reshape(outs, ins, 2, 4, 4, 9), (5, 0, 1, 2, 3, 4))

    return (
        out.reshape(source.shape),
        jnp.transpose(coarse.reshape(2, 1, 1, LX // BLK, NNULL), (0, 4, 1, 2, 3)),
        as_weights(first, 2, 1),
        as_weights(second, 1, 2),
    )


def solution(mesh):
    sizes = (mesh.shape["ta"], mesh.shape["gz"], mesh.shape["gy"])
    in_specs = (
        P(None, None, None, "ta", "gz", "gy"),
        P(None, None, None, None, "ta", "gz", "gy"),
        P(None, None, None, None, "ta", "gz", "gy"),
        P(),
        P(),
    )
    out_specs = (P(None, None, None, "ta", "gz", "gy"), P(None, None, "ta", "gz", "gy"), P(), P())
    return jax.shard_map(
        functools.partial(body, sizes),
        mesh=mesh,
        in_specs=in_specs,
        out_specs=out_specs,
        check_vma=False,
    )
```

```python
import functools

import jax
import jax.numpy as jnp
import numpy as np
from jax import lax
from jax.experimental import pallas as pl
from jax.experimental.pallas import tpu as pltpu
from jax.sharding import PartitionSpec as P

BLK = 4
NNULL = 24
LT = 4
LZ = 4
LX = 32
LANES = 128
ROWS = LT * LZ
WIDE = LZ * 3 * LANES
STACK = 80
BARE_MASS = -0.5
MESH = pl.DeviceIdType.MESH
F32 = jnp.float32
BF16 = jnp.bfloat16


def dirac_matrix():
    paulis = [
        np.array([[0, 1], [1, 0]], dtype=complex),
        np.array([[0, -1j], [1j, 0]], dtype=complex),
        np.array([[1, 0], [0, -1]], dtype=complex),
    ]
    corners = [-1j * matrix for matrix in paulis] + [np.eye(2, dtype=complex)]
    terms = [(4.0 + BARE_MASS) * np.eye(4)]
    for corner in corners:
        gamma = np.zeros((4, 4), dtype=complex)
        gamma[:2, 2:] = corner
        gamma[2:, :2] = corner.conj().T
        terms.append(-0.5 * (np.eye(4) - gamma))
        terms.append(-0.5 * (np.eye(4) + gamma))
    whole = np.zeros((16, STACK), dtype=np.float32)
    for path, term in enumerate(terms):
        block = np.block([[term.real, -term.imag], [term.imag, term.real]])
        whole[:8, path * 8 : path * 8 + 8] = block
    return np.concatenate([whole, whole], axis=1)


def index_maps(width):
    row = lax.broadcasted_iota(jnp.int32, (128, width), 0)
    col = lax.broadcasted_iota(jnp.int32, (128, width), 1)
    mask = jnp.where(row < 64, row % 4, row // 4 % 4) == col % 4
    return mask, col // 4 % 2


def left_maps(shape, row_dim, mat_dim):
    row = lax.broadcasted_iota(jnp.int32, shape, row_dim)
    mat = lax.broadcasted_iota(jnp.int32, shape, mat_dim)
    first = row < 64
    part, part_mat = row // 16 % 2, mat // 4 % 2
    match = jnp.logical_and(row // 32 == mat // 8, jnp.where(first, row // 4 % 4, row % 4) == mat % 4)
    same = part == part_mat
    sign_same = jnp.where(jnp.logical_or(first, part_mat == 0), 1.0, -1.0)
    sign_cross = jnp.where(jnp.logical_and(first, part_mat == 0), -1.0, 1.0)
    keep = jnp.where(jnp.logical_and(match, same), sign_same, 0.0).astype(F32)
    swap = jnp.where(jnp.logical_and(match, jnp.logical_not(same)), sign_cross, 0.0).astype(F32)
    return keep, swap


def exact_dot(left, right):
    return jnp.dot(left, right, precision=lax.Precision.HIGHEST, preferred_element_type=F32)


def spread_weights(values):
    width = 2 * STACK
    row = lax.broadcasted_iota(jnp.int32, (9, width), 0)
    col = lax.broadcasted_iota(jnp.int32, (9, width), 1)
    path = (row == jnp.where(col >= STACK, col - STACK, col) // 8).astype(F32)
    wide = exact_dot(values, path)
    mask, kind = index_maps(width)
    keep, swap = left_maps((32, 128), 1, 0)
    wide = jnp.where(mask, wide, 0.0)
    straight = jnp.where(kind == 0, wide, 0.0)
    return exact_dot(keep, straight) + exact_dot(swap, wide - straight)


def gather_weights(product):
    keep, swap = left_maps((128, 32), 0, 1)
    mask, kind = index_maps(STACK)
    wide = jnp.where(kind == 0, exact_dot(keep, product), exact_dot(swap, product))
    wide = jnp.where(mask, wide, 0.0)
    row = lax.broadcasted_iota(jnp.int32, (STACK, 9), 0)
    col = lax.broadcasted_iota(jnp.int32, (STACK, 9), 1)
    return exact_dot(wide, (row // 8 == col).astype(F32))


def kernel(
    sizes,
    source_hbm,
    links_hbm,
    null_hbm,
    w_first_hbm,
    w_second_hbm,
    dirac_hbm,
    out_ref,
    coarse_ref,
    weight_ref,
    source_ref,
    links_ref,
    null_ref,
    w_ref,
    dirac_ref,
    first_ref,
    second_ref,
    back_ref,
    grad_ref,
    out_face,
    in_face,
    dy,
    field,
    stack,
    x_first,
    hid,
    mixed,
    total,
    miss,
    cot,
    sums,
    spread_ref,
    red_y,
    red_t,
    send_sem,
    recv_sem,
    red_send,
    red_recv,
    load_sem,
):
    nt, nz, ny = sizes
    it = lax.axis_index("ta")
    iz = lax.axis_index("gz")
    iy = lax.axis_index("gy")
    link_rows = 18 * ROWS

    def link_slice(ref, mu):
        return ref.at[pl.ds(mu * link_rows, link_rows), :]

    loads = [
        (source_hbm, source_ref),
        (link_slice(links_hbm, 1), link_slice(links_ref, 1)),
        (link_slice(links_hbm, 3), link_slice(links_ref, 3)),
        (link_slice(links_hbm, 2), link_slice(links_ref, 2)),
        (link_slice(links_hbm, 0), link_slice(links_ref, 0)),
        (dirac_hbm, dirac_ref),
        (w_first_hbm, w_ref.at[0]),
        (w_second_hbm, w_ref.at[1]),
        (null_hbm, null_ref),
    ]
    loads = [
        pltpu.make_async_copy(src, dst, load_sem.at[k]) for k, (src, dst) in enumerate(loads)
    ]
    for load in loads:
        load.start()
    null_copy = loads.pop()

    barrier = pltpu.get_barrier_semaphore()
    plane = [
        {"gz": lax.rem(iz + a, nz), "gy": lax.rem(iy + b, ny)}
        for a in range(nz)
        for b in range(ny)
    ][1:]
    column_of = [{"ta": lax.rem(it + a, nt)} for a in range(1, nt)]
    for partner in plane + column_of:
        pl.semaphore_signal(barrier, inc=1, device_id=partner, device_id_type=MESH)
    pl.semaphore_wait(barrier, len(plane) + len(column_of))

    row_id = lax.broadcasted_iota(jnp.int32, (8, LANES), 0)
    lane = lax.broadcasted_iota(jnp.int32, (8, LANES), 1)
    column = lane % LX
    sign = jnp.where(row_id < 4, -1.0, 1.0).astype(F32)
    wrap = it == nt - 1

    def link(mu, t, z):
        row = t * LZ + z
        held = {}

        def part(which, a, b):
            if (which, a, b) not in held:
                base = ((mu * 2 + which) * 9 + a * 3 + b) * ROWS
                held[which, a, b] = jnp.broadcast_to(
                    links_ref[pl.ds(base + row, 1), :], (8, LANES)
                )
            return held[which, a, b]

        return part

    def turned(values):
        return [pltpu.roll(v, 4, 0) * sign for v in values]

    def time_edge(values):
        factor = jnp.where(wrap, -1.0, 1.0).astype(F32)
        return [v * factor for v in values]

    def forward(part, values):
        spun = turned(values)
        outs = []
        for a in range(3):
            acc = None
            for b in range(3):
                term = part(0, a, b) * values[b] + part(1, a, b) * spun[b]
                acc = term if acc is None else acc + term
            outs.append(acc)
        return outs

    def adjoint(part, values):
        spun = turned(values)
        outs = []
        for a in range(3):
            acc = None
            for b in range(3):
                term = part(0, b, a) * values[b] - part(1, b, a) * spun[b]
                acc = term if acc is None else acc + term
            outs.append(acc)
        return outs

    def over_time(body, count=LT):
        def step(t, carry):
            body(t)
            return carry

        lax.fori_loop(0, count, step, 0)

    def exchange(rd, src_up, src_dn, put, meanwhile=None, ready=None):
        def send(which, axis, target):
            copy = pltpu.make_async_remote_copy(
                src_ref=out_face.at[rd, which],
                dst_ref=in_face.at[rd, which],
                send_sem=send_sem.at[rd, which],
                recv_sem=recv_sem.at[rd, which],
                device_id={axis: target},
                device_id_type=MESH,
            )
            copy.start()
            return copy

        def quarters(values, shift):
            a, b, c, d = [
                pltpu.roll(v, (32 * k + shift) % LANES, 1) if (32 * k + shift) % LANES else v
                for k, v in enumerate(values)
            ]
            return jnp.where(
                lane < 64, jnp.where(lane < 32, a, b), jnp.where(lane < 96, c, d)
            )

        def unpacked(which, t, c, z, shift):
            value = in_face[rd, which, t, c]
            amount = (-32 * z - shift) % LANES
            return pltpu.roll(value, amount, 1) if amount else value

        def y_up(t):
            ups = [src_up(1, t, z) for z in range(LZ)]
            for c in range(3):
                out_face[rd, 0, t, c] = quarters([up[c] for up in ups], 0)

        def y_down(t):
            downs = [adjoint(link(1, t, z), src_dn(1, t, z)) for z in range(LZ)]
            for c in range(3):
                for z in range(LZ):
                    dy[t, z, c] = downs[z][c]
                out_face[rd, 3, t, c] = quarters([down[c] for down in downs], 32)

        other = lax.rem(iy + 1, ny)
        t_before, t_after = lax.rem(it + nt - 1, nt), lax.rem(it + 1, nt)
        z_before, z_after = lax.rem(iz + nz - 1, nz), lax.rem(iz + 1, nz)
        over_time(y_up)
        c_yu = send(0, "gy", other)
        for z in range(LZ):
            values = src_up(3, 0, z)
            for c in range(3):
                out_face[rd, 1, z, c] = values[c]
        c_tu = send(1, "ta", t_before)
        for t in range(LT):
            values = src_up(2, t, 0)
            for c in range(3):
                out_face[rd, 2, t, c] = values[c]
        c_zu = send(2, "gz", z_before)
        if ready is not None:
            ready(1)
        over_time(y_down)
        c_yd = send(3, "gy", other)
        if ready is not None:
            ready(3)
        for z in range(LZ):
            values = adjoint(link(3, LT - 1, z), time_edge(src_dn(3, LT - 1, z)))
            for c in range(3):
                out_face[rd, 4, z, c] = values[c]
        c_td = send(4, "ta", t_after)
        if ready is not None:
            ready(2)

        def z_down(t):
            values = adjoint(link(2, t, LZ - 1), src_dn(2, t, LZ - 1))
            for c in range(3):
                out_face[rd, 5, t, c] = values[c]

        over_time(z_down)
        c_zd = send(5, "gz", z_after)

        def t_inner(t):
            for z in range(LZ):
                part = link(3, t, z)
                put(7, t, z, forward(part, src_up(3, t + 1, z)))
                put(8, t + 1, z, adjoint(part, src_dn(3, t, z)))

        over_time(t_inner, LT - 1)

        def z_inner(t):
            for z in range(LZ - 1):
                part = link(2, t, z)
                put(5, t, z, forward(part, src_up(2, t, z + 1)))
                put(6, t, z + 1, adjoint(part, src_dn(2, t, z)))

        over_time(z_inner)
        if ready is not None:
            ready(0)

        def x_part(t):
            for z in range(LZ):
                part = link(0, t, z)
                up = [
                    jnp.where(column == LX - 1, pltpu.roll(v, LX - 1, 1), pltpu.roll(v, LANES - 1, 1))
                    for v in src_up(0, t, z)
                ]
                put(1, t, z, forward(part, up))
                down = [
                    jnp.where(column == 0, pltpu.roll(v, LANES + 1 - LX, 1), pltpu.roll(v, 1, 1))
                    for v in adjoint(part, src_dn(0, t, z))
                ]
                put(2, t, z, down)

        over_time(x_part)
        if meanwhile is not None:
            meanwhile()
        c_yu.wait()

        def y_up_take(t):
            for z in range(LZ):
                up = [
                    pltpu.roll(jnp.where(lane < 32, unpacked(0, t, c, z, 0), v), 96, 1)
                    for c, v in enumerate(src_up(1, t, z))
                ]
                put(3, t, z, forward(link(1, t, z), up))

        over_time(y_up_take)
        c_tu.wait()
        for z in range(LZ):
            up = time_edge([in_face[rd, 1, z, c] for c in range(3)])
            put(7, LT - 1, z, forward(link(3, LT - 1, z), up))
        c_zu.wait()

        def z_up_take(t):
            up = [in_face[rd, 2, t, c] for c in range(3)]
            put(5, t, LZ - 1, forward(link(2, t, LZ - 1), up))

        over_time(z_up_take)
        c_yd.wait()

        def y_down_take(t):
            for z in range(LZ):
                down = [
                    pltpu.roll(jnp.where(lane >= 96, unpacked(3, t, c, z, 32), dy[t, z, c]), 32, 1)
                    for c in range(3)
                ]
                put(4, t, z, down)

        over_time(y_down_take)
        c_td.wait()
        for z in range(LZ):
            put(8, 0, z, [in_face[rd, 4, z, c] for c in range(3)])
        c_zd.wait()
        for t in range(LT):
            put(6, t, 0, [in_face[rd, 5, t, c] for c in range(3)])

    def from_field(mu, t, z):
        return [field[t, z, c] for c in range(3)]

    def put_stack(path, t, z, values):
        for c in range(3):
            stack[t, z, c, path * 8 : path * 8 + 8, :] = values[c]

    def put_swapped(path, t, z, values):
        put_stack(path + 1 if path % 2 == 1 else path - 1, t, z, values)

    def split(values):
        high = values.astype(BF16)
        low = (values - high.astype(F32)).astype(BF16)
        return jnp.concatenate([high, low], axis=0)

    def identity_path():
        def step(t):
            for z in range(LZ):
                for c in range(3):
                    stack[t, z, c, 0:8, :] = field[t, z, c]

        over_time(step)

    def stacked_columns(t):
        return jnp.concatenate(
            [split(stack[t, z, c]) for z in range(LZ) for c in range(3)], axis=1
        )

    def dot(left, right):
        return lax.dot_general(
            left, right, (((1,), (0,)), ((), ())), preferred_element_type=F32
        )

    def dot_t(left, right):
        return lax.dot_general(
            left, right, (((1,), (1,)), ((), ())), preferred_element_type=F32
        )

    def load_source(ref):
        def step(t):
            for z in range(LZ):
                for c in range(3):
                    field[t, z, c] = ref[pl.ds(c * ROWS + t * LZ + z, 8, stride=3 * ROWS), :]

        over_time(step)

    def clear(t):
        for z in range(LZ):
            for c in range(3):
                stack[t, z, c, 72:80, :] = jnp.zeros((8, LANES), F32)

    over_time(clear)

    def prepare():
        for load in loads[5:]:
            load.wait()
        values = spread_weights(w_ref[...].reshape(128, 9))
        high = values.astype(BF16)
        low = values - high.astype(F32)
        low = low.astype(BF16)
        first_ref[...] = jnp.concatenate([high[0:16], low[0:16]], axis=0)
        back_ref[...] = jnp.concatenate([high[16:32], low[16:32]], axis=0)
        col = lax.broadcasted_iota(jnp.int32, (16, 2 * STACK), 1)
        mixing = jnp.where(col < STACK, high[16:32].astype(F32), low[16:32].astype(F32))
        mixing = jnp.concatenate([mixing, mixing], axis=0)
        second_ref[...] = jnp.transpose(mixing).astype(BF16)

    loads[0].wait()
    load_source(source_ref)
    identity_path()

    def ready(mu):
        loads[(4, 1, 3, 2)[mu]].wait()

    exchange(0, from_field, from_field, put_stack, prepare, ready)

    def residual_step(t):
        result = dot(dirac_ref[...].astype(BF16), stacked_columns(t))
        for z in range(LZ):
            for c in range(3):
                j = (z * 3 + c) * LANES
                field[t, z, c] = result[0:8, j : j + LANES]

    over_time(residual_step)

    identity_path()
    exchange(1, from_field, from_field, put_stack)

    def hidden_step(t):
        columns = stacked_columns(t)
        x_first[t] = columns
        result = dot(first_ref[...], columns)
        hid[t] = split(result[0:16] + result[16:32])
        product = dot(second_ref[...], hid[t])
        product = product[0:STACK] + product[STACK : 2 * STACK]
        for z in range(LZ):
            for c in range(3):
                j = (z * 3 + c) * LANES
                mixed[t, z, c] = product[:, j : j + LANES]
                total[t, z, c] = product[0:8, j : j + LANES]

    over_time(hidden_step)

    def mixed_up(mu, t, z):
        k = (1 + 2 * mu) * 8
        return [mixed[t, z, c, k : k + 8, :] for c in range(3)]

    def mixed_dn(mu, t, z):
        k = (2 + 2 * mu) * 8
        return [mixed[t, z, c, k : k + 8, :] for c in range(3)]

    def put_total(path, t, z, values):
        for c in range(3):
            total[t, z, c] += values[c]

    exchange(2, mixed_up, mixed_dn, put_total)

    def store_out(t):
        for z in range(LZ):
            for c in range(3):
                out_ref[pl.ds(c * ROWS + t * LZ + z, 8, stride=3 * ROWS), :] = total[t, z, c]

    over_time(store_out)
    miss[...] = out_ref[...] - source_ref[...]
    null_copy.wait()

    def restrict_step(k, carry):
        re = jnp.zeros((ROWS, LANES), F32)
        im = jnp.zeros((ROWS, LANES), F32)
        for j in range(12):
            v_re = null_ref[pl.ds(pl.multiple_of((k * 24 + j) * ROWS, ROWS), ROWS), :].astype(F32)
            v_im = null_ref[
                pl.ds(pl.multiple_of((k * 24 + 12 + j) * ROWS, ROWS), ROWS), :
            ].astype(F32)
            m_re = miss[j * ROWS : (j + 1) * ROWS, :]
            m_im = miss[(12 + j) * ROWS : (13 + j) * ROWS, :]
            re = re + (v_re * m_re + v_im * m_im)
            im = im + (v_re * m_im - v_im * m_re)
        sums[pl.ds(k, 1), :] = jnp.sum(re, axis=0, keepdims=True)
        sums[pl.ds(NNULL + k, 1), :] = jnp.sum(im, axis=0, keepdims=True)
        return carry

    lax.fori_loop(0, NNULL, restrict_step, 0)
    left = lax.broadcasted_iota(jnp.int32, (LANES, LANES), 0) % LX // BLK
    right = lax.broadcasted_iota(jnp.int32, (LANES, LANES), 1) % LX // BLK
    spread_ref[...] = exact_dot(sums[...], (left == right).astype(F32))
    block = lax.broadcasted_iota(jnp.int32, (8, LANES), 0)
    pick = (block == column // BLK).astype(F32)
    for half in range(2):
        coarse_ref[half * 8 : half * 8 + 8, :] = lax.dot_general(
            pick,
            sums[half * NNULL : (half + 1) * NNULL, :],
            (((1,), (1,)), ((), ())),
            precision=lax.Precision.HIGHEST,
            preferred_element_type=F32,
        )

    scale = 2.0 / (ROWS * LANES * nt * nz * ny)

    def prolong_step(j, carry):
        re = miss[pl.ds(pl.multiple_of(j * ROWS, ROWS), ROWS), :]
        im = miss[pl.ds(pl.multiple_of((12 + j) * ROWS, ROWS), ROWS), :]
        for k in range(NNULL):
            v_re = null_ref[pl.ds(pl.multiple_of((k * 24 + j) * ROWS, ROWS), ROWS), :].astype(F32)
            v_im = null_ref[
                pl.ds(pl.multiple_of((k * 24 + 12 + j) * ROWS, ROWS), ROWS), :
            ].astype(F32)
            s_re = spread_ref[k : k + 1, :]
            s_im = spread_ref[NNULL + k : NNULL + k + 1, :]
            re = re + (s_re * v_re - s_im * v_im)
            im = im + (s_re * v_im + s_im * v_re)
        cot[pl.ds(pl.multiple_of(j * ROWS, ROWS), ROWS), :] = re * scale
        cot[pl.ds(pl.multiple_of((12 + j) * ROWS, ROWS), ROWS), :] = im * scale
        return carry

    lax.fori_loop(0, 12, prolong_step, 0)

    load_source(cot)
    identity_path()
    exchange(3, from_field, from_field, put_swapped)

    def back_step(t, carry):
        first_sum, second_sum = carry
        columns = stacked_columns(t)
        result = dot(back_ref[...], columns)
        back = split(result[0:16] + result[16:32])
        first_cols = x_first[t]
        g1 = dot_t(back, first_cols[0:STACK]) + dot_t(back, first_cols[STACK : 2 * STACK])
        g2 = dot_t(hid[t], columns[0:STACK]) + dot_t(hid[t], columns[STACK : 2 * STACK])
        return first_sum + g1[0:16] + g1[16:32], second_sum + g2[0:16] + g2[16:32]

    zero = jnp.zeros((16, STACK), F32)
    first_sum, second_sum = lax.fori_loop(0, LT, back_step, (zero, zero))

    grad_ref[...] = jnp.zeros_like(grad_ref)
    grad_ref[0:16, 0:STACK] = first_sum
    grad_ref[16:32, 0:STACK] = second_sum
    base = 0
    for partners, mine, slots in ((plane, iz * ny + iy, red_y), (column_of, it, red_t)):
        slots[mine] = grad_ref[...]
        copies = []
        for step, partner in enumerate(partners):
            copy = pltpu.make_async_remote_copy(
                src_ref=slots.at[mine],
                dst_ref=slots.at[mine],
                send_sem=red_send.at[base + step],
                recv_sem=red_recv.at[base + step],
                device_id=partner,
                device_id_type=MESH,
            )
            copy.start()
            copies.append(copy)
        for copy in copies:
            copy.wait()
        acc = slots[0]
        for j in range(1, len(partners) + 1):
            acc = acc + slots[j]
        grad_ref[...] = acc
        base += len(partners)
    weight_ref[...] = gather_weights(grad_ref[:, 0:STACK])


def store_kernel(out_ref, coarse_ref, weight_ref, out_hbm, coarse_hbm, first_hbm, second_hbm, sem):
    pairs = [
        (out_ref, out_hbm),
        (coarse_ref, coarse_hbm),
        (weight_ref.at[0:64, :], first_hbm),
        (weight_ref.at[64:128, :], second_hbm),
    ]
    copies = [pltpu.make_async_copy(src, dst, sem.at[k]) for k, (src, dst) in enumerate(pairs)]
    for copy in copies:
        copy.start()
    for copy in copies:
        copy.wait()


def body(sizes, source, gauge_links, near_null, w_first, w_second):
    nt, nz, ny = sizes
    vmem = pl.BlockSpec(memory_space=pltpu.VMEM)
    slab = (3, 8, LANES)
    hbm = pl.BlockSpec(memory_space=pltpu.HBM)
    out, coarse, grad = pl.pallas_call(
        functools.partial(kernel, sizes),
        out_shape=(
            jax.ShapeDtypeStruct((24 * ROWS, LANES), F32),
            jax.ShapeDtypeStruct((16, NNULL), F32),
            jax.ShapeDtypeStruct((128, 9), F32),
        ),
        in_specs=[hbm] * 6,
        out_specs=(vmem, vmem, vmem),
        scratch_shapes=[
            pltpu.VMEM((24 * ROWS, LANES), F32),
            pltpu.VMEM((72 * ROWS, LANES), F32),
            pltpu.VMEM((NNULL * 24 * ROWS, LANES), BF16),
            pltpu.VMEM((2, 64, 9), F32),
            pltpu.VMEM((16, 2 * STACK), F32),
            pltpu.VMEM((32, 2 * STACK), BF16),
            pltpu.VMEM((2 * STACK, 32), BF16),
            pltpu.VMEM((32, 2 * STACK), BF16),
            pltpu.VMEM((32, LANES), F32),
            pltpu.VMEM((4, 6, 4) + slab, F32),
            pltpu.VMEM((4, 6, 4) + slab, F32),
            pltpu.VMEM((LT, LZ) + slab, F32),
            pltpu.VMEM((LT, LZ) + slab, F32),
            pltpu.VMEM((LT, LZ, 3, STACK, LANES), F32),
            pltpu.VMEM((LT, 2 * STACK, WIDE), BF16),
            pltpu.VMEM((LT, 32, WIDE), BF16),
            pltpu.VMEM((LT, LZ, 3, STACK, LANES), F32),
            pltpu.VMEM((LT, LZ) + slab, F32),
            pltpu.VMEM((24 * ROWS, LANES), F32),
            pltpu.VMEM((24 * ROWS, LANES), F32),
            pltpu.VMEM((2 * NNULL, LANES), F32),
            pltpu.VMEM((2 * NNULL, LANES), F32),
            pltpu.VMEM((ny * nz, 32, LANES), F32),
            pltpu.VMEM((nt, 32, LANES), F32),
            pltpu.SemaphoreType.DMA((4, 6)),
            pltpu.SemaphoreType.DMA((4, 6)),
            pltpu.SemaphoreType.DMA((nt + nz * ny,)),
            pltpu.SemaphoreType.DMA((nt + nz * ny,)),
            pltpu.SemaphoreType.DMA((9,)),
        ],
        compiler_params=pltpu.CompilerParams(
            collective_id=0, has_side_effects=True, vmem_limit_bytes=(65536 - 288) * 1024
        ),
    )(
        source.reshape(24 * ROWS, LANES),
        gauge_links.reshape(72 * ROWS, LANES),
        near_null.reshape(NNULL * 24 * ROWS, LANES),
        jnp.transpose(w_first, (1, 2, 3, 4, 5, 0)).reshape(64, 9),
        jnp.transpose(w_second, (1, 2, 3, 4, 5, 0)).reshape(64, 9),
        jnp.asarray(dirac_matrix()),
    )
    out, coarse, first, second = pl.pallas_call(
        store_kernel,
        out_shape=(
            jax.ShapeDtypeStruct((24 * ROWS, LANES), F32),
            jax.ShapeDtypeStruct((16, NNULL), F32),
            jax.ShapeDtypeStruct((64, 9), F32),
            jax.ShapeDtypeStruct((64, 9), F32),
        ),
        in_specs=[vmem] * 3,
        out_specs=(hbm,) * 4,
        scratch_shapes=[pltpu.SemaphoreType.DMA((4,))],
    )(out, coarse, grad)

    def as_weights(values, outs, ins):
        return jnp.transpose(values.reshape(outs, ins, 2, 4, 4, 9), (5, 0, 1, 2, 3, 4))

    return (
        out.reshape(source.shape),
        jnp.transpose(coarse.reshape(2, 1, 1, LX // BLK, NNULL), (0, 4, 1, 2, 3)),
        as_weights(first, 2, 1),
        as_weights(second, 1, 2),
    )


def solution(mesh):
    sizes = (mesh.shape["ta"], mesh.shape["gz"], mesh.shape["gy"])
    in_specs = (
        P(None, None, None, "ta", "gz", "gy"),
        P(None, None, None, None, "ta", "gz", "gy"),
        P(None, None, None, None, "ta", "gz", "gy"),
        P(),
        P(),
    )
    out_specs = (P(None, None, None, "ta", "gz", "gy"), P(None, None, "ta", "gz", "gy"), P(), P())
    return jax.shard_map(
        functools.partial(body, sizes),
        mesh=mesh,
        in_specs=in_specs,
        out_specs=out_specs,
        check_vma=False,
    )
```

```python
import functools

import jax
import jax.numpy as jnp
import numpy as np
from jax import lax
from jax.experimental import pallas as pl
from jax.experimental.pallas import tpu as pltpu
from jax.sharding import PartitionSpec as P

BLK = 4
NNULL = 24
LT = 4
LZ = 4
LX = 32
LANES = 128
ROWS = LT * LZ
WIDE = LZ * 3 * LANES
STACK = 80
BARE_MASS = -0.5
MESH = pl.DeviceIdType.MESH
F32 = jnp.float32
BF16 = jnp.bfloat16


def dirac_matrix():
    paulis = [
        np.array([[0, 1], [1, 0]], dtype=complex),
        np.array([[0, -1j], [1j, 0]], dtype=complex),
        np.array([[1, 0], [0, -1]], dtype=complex),
    ]
    corners = [-1j * matrix for matrix in paulis] + [np.eye(2, dtype=complex)]
    terms = [(4.0 + BARE_MASS) * np.eye(4)]
    for corner in corners:
        gamma = np.zeros((4, 4), dtype=complex)
        gamma[:2, 2:] = corner
        gamma[2:, :2] = corner.conj().T
        terms.append(-0.5 * (np.eye(4) - gamma))
        terms.append(-0.5 * (np.eye(4) + gamma))
    whole = np.zeros((16, STACK), dtype=np.float32)
    for path, term in enumerate(terms):
        block = np.block([[term.real, -term.imag], [term.imag, term.real]])
        whole[:8, path * 8 : path * 8 + 8] = block
    return np.concatenate([whole, whole], axis=1)


def index_maps(width):
    row = lax.broadcasted_iota(jnp.int32, (128, width), 0)
    col = lax.broadcasted_iota(jnp.int32, (128, width), 1)
    mask = jnp.where(row < 64, row % 4, row // 4 % 4) == col % 4
    return mask, col // 4 % 2


def left_maps(shape, row_dim, mat_dim):
    row = lax.broadcasted_iota(jnp.int32, shape, row_dim)
    mat = lax.broadcasted_iota(jnp.int32, shape, mat_dim)
    first = row < 64
    part, part_mat = row // 16 % 2, mat // 4 % 2
    match = jnp.logical_and(row // 32 == mat // 8, jnp.where(first, row // 4 % 4, row % 4) == mat % 4)
    same = part == part_mat
    sign_same = jnp.where(jnp.logical_or(first, part_mat == 0), 1.0, -1.0)
    sign_cross = jnp.where(jnp.logical_and(first, part_mat == 0), -1.0, 1.0)
    keep = jnp.where(jnp.logical_and(match, same), sign_same, 0.0).astype(F32)
    swap = jnp.where(jnp.logical_and(match, jnp.logical_not(same)), sign_cross, 0.0).astype(F32)
    return keep, swap


def exact_dot(left, right):
    return jnp.dot(left, right, precision=lax.Precision.HIGHEST, preferred_element_type=F32)


def spread_weights(values):
    width = 2 * STACK
    row = lax.broadcasted_iota(jnp.int32, (9, width), 0)
    col = lax.broadcasted_iota(jnp.int32, (9, width), 1)
    path = (row == jnp.where(col >= STACK, col - STACK, col) // 8).astype(F32)
    wide = exact_dot(values, path)
    mask, kind = index_maps(width)
    keep, swap = left_maps((32, 128), 1, 0)
    wide = jnp.where(mask, wide, 0.0)
    straight = jnp.where(kind == 0, wide, 0.0)
    return exact_dot(keep, straight) + exact_dot(swap, wide - straight)


def gather_weights(product):
    keep, swap = left_maps((128, 32), 0, 1)
    mask, kind = index_maps(STACK)
    wide = jnp.where(kind == 0, exact_dot(keep, product), exact_dot(swap, product))
    wide = jnp.where(mask, wide, 0.0)
    row = lax.broadcasted_iota(jnp.int32, (STACK, 9), 0)
    col = lax.broadcasted_iota(jnp.int32, (STACK, 9), 1)
    return exact_dot(wide, (row // 8 == col).astype(F32))


def kernel(
    sizes,
    source_hbm,
    links_hbm,
    null_hbm,
    w_first_hbm,
    w_second_hbm,
    dirac_hbm,
    out_ref,
    coarse_ref,
    weight_ref,
    source_ref,
    links_ref,
    null_ref,
    w_ref,
    dirac_ref,
    first_ref,
    second_ref,
    back_ref,
    grad_ref,
    out_face,
    in_face,
    dy,
    field,
    stack,
    x_first,
    hid,
    mixed,
    total,
    miss,
    cot,
    sums,
    spread_ref,
    red_y,
    red_t,
    send_sem,
    recv_sem,
    red_send,
    red_recv,
    load_sem,
):
    nt, nz, ny = sizes
    it = lax.axis_index("ta")
    iz = lax.axis_index("gz")
    iy = lax.axis_index("gy")
    link_rows = 18 * ROWS

    def link_slice(ref, mu):
        return ref.at[pl.ds(mu * link_rows, link_rows), :]

    loads = [
        (source_hbm, source_ref),
        (link_slice(links_hbm, 1), link_slice(links_ref, 1)),
        (link_slice(links_hbm, 3), link_slice(links_ref, 3)),
        (link_slice(links_hbm, 2), link_slice(links_ref, 2)),
        (link_slice(links_hbm, 0), link_slice(links_ref, 0)),
        (dirac_hbm, dirac_ref),
        (w_first_hbm, w_ref.at[0]),
        (w_second_hbm, w_ref.at[1]),
        (null_hbm, null_ref),
    ]
    loads = [
        pltpu.make_async_copy(src, dst, load_sem.at[k]) for k, (src, dst) in enumerate(loads)
    ]
    for load in loads:
        load.start()
    null_copy = loads.pop()

    barrier = pltpu.get_barrier_semaphore()
    plane = [
        {"gz": lax.rem(iz + a, nz), "gy": lax.rem(iy + b, ny)}
        for a in range(nz)
        for b in range(ny)
    ][1:]
    column_of = [{"ta": lax.rem(it + a, nt)} for a in range(1, nt)]
    for partner in plane + column_of:
        pl.semaphore_signal(barrier, inc=1, device_id=partner, device_id_type=MESH)
    pl.semaphore_wait(barrier, len(plane) + len(column_of))

    row_id = lax.broadcasted_iota(jnp.int32, (8, LANES), 0)
    lane = lax.broadcasted_iota(jnp.int32, (8, LANES), 1)
    column = lane % LX
    sign = jnp.where(row_id < 4, -1.0, 1.0).astype(F32)
    wrap = it == nt - 1

    def link(mu, t, z):
        row = t * LZ + z
        held = {}

        def part(which, a, b):
            if (which, a, b) not in held:
                base = ((mu * 2 + which) * 9 + a * 3 + b) * ROWS
                held[which, a, b] = jnp.broadcast_to(
                    links_ref[pl.ds(base + row, 1), :], (8, LANES)
                )
            return held[which, a, b]

        return part

    def turned(values):
        return [pltpu.roll(v, 4, 0) * sign for v in values]

    def time_edge(values):
        factor = jnp.where(wrap, -1.0, 1.0).astype(F32)
        return [v * factor for v in values]

    def forward(part, values):
        spun = turned(values)
        outs = []
        for a in range(3):
            acc = None
            for b in range(3):
                term = part(0, a, b) * values[b] + part(1, a, b) * spun[b]
                acc = term if acc is None else acc + term
            outs.append(acc)
        return outs

    def adjoint(part, values):
        spun = turned(values)
        outs = []
        for a in range(3):
            acc = None
            for b in range(3):
                term = part(0, b, a) * values[b] - part(1, b, a) * spun[b]
                acc = term if acc is None else acc + term
            outs.append(acc)
        return outs

    def over_time(body, count=LT):
        def step(t, carry):
            body(t)
            return carry

        lax.fori_loop(0, count, step, 0, unroll=True)

    def exchange(rd, src_up, src_dn, put, meanwhile=None, ready=None):
        def send(which, axis, target):
            copy = pltpu.make_async_remote_copy(
                src_ref=out_face.at[rd, which],
                dst_ref=in_face.at[rd, which],
                send_sem=send_sem.at[rd, which],
                recv_sem=recv_sem.at[rd, which],
                device_id={axis: target},
                device_id_type=MESH,
            )
            copy.start()
            return copy

        def quarters(values, shift):
            a, b, c, d = [
                pltpu.roll(v, (32 * k + shift) % LANES, 1) if (32 * k + shift) % LANES else v
                for k, v in enumerate(values)
            ]
            return jnp.where(
                lane < 64, jnp.where(lane < 32, a, b), jnp.where(lane < 96, c, d)
            )

        def unpacked(which, t, c, z, shift):
            value = in_face[rd, which, t, c]
            amount = (-32 * z - shift) % LANES
            return pltpu.roll(value, amount, 1) if amount else value

        def y_up(t):
            ups = [src_up(1, t, z) for z in range(LZ)]
            for c in range(3):
                out_face[rd, 0, t, c] = quarters([up[c] for up in ups], 0)

        def y_down(t):
            downs = [adjoint(link(1, t, z), src_dn(1, t, z)) for z in range(LZ)]
            for c in range(3):
                for z in range(LZ):
                    dy[t, z, c] = downs[z][c]
                out_face[rd, 3, t, c] = quarters([down[c] for down in downs], 32)

        other = lax.rem(iy + 1, ny)
        t_before, t_after = lax.rem(it + nt - 1, nt), lax.rem(it + 1, nt)
        z_before, z_after = lax.rem(iz + nz - 1, nz), lax.rem(iz + 1, nz)
        over_time(y_up)
        c_yu = send(0, "gy", other)
        for z in range(LZ):
            values = src_up(3, 0, z)
            for c in range(3):
                out_face[rd, 1, z, c] = values[c]
        c_tu = send(1, "ta", t_before)
        for t in range(LT):
            values = src_up(2, t, 0)
            for c in range(3):
                out_face[rd, 2, t, c] = values[c]
        c_zu = send(2, "gz", z_before)
        if ready is not None:
            ready(1)
        over_time(y_down)
        c_yd = send(3, "gy", other)
        if ready is not None:
            ready(3)
        for z in range(LZ):
            values = adjoint(link(3, LT - 1, z), time_edge(src_dn(3, LT - 1, z)))
            for c in range(3):
                out_face[rd, 4, z, c] = values[c]
        c_td = send(4, "ta", t_after)
        if ready is not None:
            ready(2)

        def z_down(t):
            values = adjoint(link(2, t, LZ - 1), src_dn(2, t, LZ - 1))
            for c in range(3):
                out_face[rd, 5, t, c] = values[c]

        over_time(z_down)
        c_zd = send(5, "gz", z_after)

        def t_inner(t):
            for z in range(LZ):
                part = link(3, t, z)
                put(7, t, z, forward(part, src_up(3, t + 1, z)))
                put(8, t + 1, z, adjoint(part, src_dn(3, t, z)))

        over_time(t_inner, LT - 1)

        def z_inner(t):
            for z in range(LZ - 1):
                part = link(2, t, z)
                put(5, t, z, forward(part, src_up(2, t, z + 1)))
                put(6, t, z + 1, adjoint(part, src_dn(2, t, z)))

        over_time(z_inner)
        if ready is not None:
            ready(0)

        def x_part(t):
            for z in range(LZ):
                part = link(0, t, z)
                up = [
                    jnp.where(column == LX - 1, pltpu.roll(v, LX - 1, 1), pltpu.roll(v, LANES - 1, 1))
                    for v in src_up(0, t, z)
                ]
                put(1, t, z, forward(part, up))
                down = [
                    jnp.where(column == 0, pltpu.roll(v, LANES + 1 - LX, 1), pltpu.roll(v, 1, 1))
                    for v in adjoint(part, src_dn(0, t, z))
                ]
                put(2, t, z, down)

        over_time(x_part)
        if meanwhile is not None:
            meanwhile()
        c_yu.wait()

        def y_up_take(t):
            for z in range(LZ):
                up = [
                    pltpu.roll(jnp.where(lane < 32, unpacked(0, t, c, z, 0), v), 96, 1)
                    for c, v in enumerate(src_up(1, t, z))
                ]
                put(3, t, z, forward(link(1, t, z), up))

        over_time(y_up_take)
        c_tu.wait()
        for z in range(LZ):
            up = time_edge([in_face[rd, 1, z, c] for c in range(3)])
            put(7, LT - 1, z, forward(link(3, LT - 1, z), up))
        c_zu.wait()

        def z_up_take(t):
            up = [in_face[rd, 2, t, c] for c in range(3)]
            put(5, t, LZ - 1, forward(link(2, t, LZ - 1), up))

        over_time(z_up_take)
        c_yd.wait()

        def y_down_take(t):
            for z in range(LZ):
                down = [
                    pltpu.roll(jnp.where(lane >= 96, unpacked(3, t, c, z, 32), dy[t, z, c]), 32, 1)
                    for c in range(3)
                ]
                put(4, t, z, down)

        over_time(y_down_take)
        c_td.wait()
        for z in range(LZ):
            put(8, 0, z, [in_face[rd, 4, z, c] for c in range(3)])
        c_zd.wait()
        for t in range(LT):
            put(6, t, 0, [in_face[rd, 5, t, c] for c in range(3)])

    def from_field(mu, t, z):
        return [field[t, z, c] for c in range(3)]

    def put_stack(path, t, z, values):
        for c in range(3):
            stack[t, z, c, path * 8 : path * 8 + 8, :] = values[c]

    def put_swapped(path, t, z, values):
        put_stack(path + 1 if path % 2 == 1 else path - 1, t, z, values)

    def split(values):
        high = values.astype(BF16)
        low = (values - high.astype(F32)).astype(BF16)
        return jnp.concatenate([high, low], axis=0)

    def identity_path():
        def step(t):
            for z in range(LZ):
                for c in range(3):
                    stack[t, z, c, 0:8, :] = field[t, z, c]

        over_time(step)

    def stacked_columns(t):
        return jnp.concatenate(
            [split(stack[t, z, c]) for z in range(LZ) for c in range(3)], axis=1
        )

    def dot(left, right):
        return lax.dot_general(
            left, right, (((1,), (0,)), ((), ())), preferred_element_type=F32
        )

    def dot_t(left, right):
        return lax.dot_general(
            left, right, (((1,), (1,)), ((), ())), preferred_element_type=F32
        )

    def load_source(ref):
        def step(t):
            for z in range(LZ):
                for c in range(3):
                    field[t, z, c] = ref[pl.ds(c * ROWS + t * LZ + z, 8, stride=3 * ROWS), :]

        over_time(step)

    def clear(t):
        for z in range(LZ):
            for c in range(3):
                stack[t, z, c, 72:80, :] = jnp.zeros((8, LANES), F32)

    over_time(clear)

    def prepare():
        for load in loads[5:]:
            load.wait()
        values = spread_weights(w_ref[...].reshape(128, 9))
        high = values.astype(BF16)
        low = values - high.astype(F32)
        low = low.astype(BF16)
        first_ref[...] = jnp.concatenate([high[0:16], low[0:16]], axis=0)
        back_ref[...] = jnp.concatenate([high[16:32], low[16:32]], axis=0)
        col = lax.broadcasted_iota(jnp.int32, (16, 2 * STACK), 1)
        mixing = jnp.where(col < STACK, high[16:32].astype(F32), low[16:32].astype(F32))
        mixing = jnp.concatenate([mixing, mixing], axis=0)
        second_ref[...] = jnp.transpose(mixing).astype(BF16)

    loads[0].wait()
    load_source(source_ref)
    identity_path()

    def ready(mu):
        loads[(4, 1, 3, 2)[mu]].wait()

    exchange(0, from_field, from_field, put_stack, prepare, ready)

    def residual_step(t):
        result = dot(dirac_ref[...].astype(BF16), stacked_columns(t))
        for z in range(LZ):
            for c in range(3):
                j = (z * 3 + c) * LANES
                field[t, z, c] = result[0:8, j : j + LANES]

    over_time(residual_step)

    identity_path()
    exchange(1, from_field, from_field, put_stack)

    def hidden_step(t):
        columns = stacked_columns(t)
        x_first[t] = columns
        result = dot(first_ref[...], columns)
        hid[t] = split(result[0:16] + result[16:32])
        product = dot(second_ref[...], hid[t])
        product = product[0:STACK] + product[STACK : 2 * STACK]
        for z in range(LZ):
            for c in range(3):
                j = (z * 3 + c) * LANES
                mixed[t, z, c] = product[:, j : j + LANES]
                total[t, z, c] = product[0:8, j : j + LANES]

    over_time(hidden_step)

    def mixed_up(mu, t, z):
        k = (1 + 2 * mu) * 8
        return [mixed[t, z, c, k : k + 8, :] for c in range(3)]

    def mixed_dn(mu, t, z):
        k = (2 + 2 * mu) * 8
        return [mixed[t, z, c, k : k + 8, :] for c in range(3)]

    def put_total(path, t, z, values):
        for c in range(3):
            total[t, z, c] += values[c]

    exchange(2, mixed_up, mixed_dn, put_total)

    def store_out(t):
        for z in range(LZ):
            for c in range(3):
                out_ref[pl.ds(c * ROWS + t * LZ + z, 8, stride=3 * ROWS), :] = total[t, z, c]

    over_time(store_out)
    miss[...] = out_ref[...] - source_ref[...]
    null_copy.wait()

    def restrict_step(k, carry):
        re = jnp.zeros((ROWS, LANES), F32)
        im = jnp.zeros((ROWS, LANES), F32)
        for j in range(12):
            v_re = null_ref[pl.ds(pl.multiple_of((k * 24 + j) * ROWS, ROWS), ROWS), :].astype(F32)
            v_im = null_ref[
                pl.ds(pl.multiple_of((k * 24 + 12 + j) * ROWS, ROWS), ROWS), :
            ].astype(F32)
            m_re = miss[j * ROWS : (j + 1) * ROWS, :]
            m_im = miss[(12 + j) * ROWS : (13 + j) * ROWS, :]
            re = re + (v_re * m_re + v_im * m_im)
            im = im + (v_re * m_im - v_im * m_re)
        sums[pl.ds(k, 1), :] = jnp.sum(re, axis=0, keepdims=True)
        sums[pl.ds(NNULL + k, 1), :] = jnp.sum(im, axis=0, keepdims=True)
        return carry

    lax.fori_loop(0, NNULL, restrict_step, 0)
    left = lax.broadcasted_iota(jnp.int32, (LANES, LANES), 0) % LX // BLK
    right = lax.broadcasted_iota(jnp.int32, (LANES, LANES), 1) % LX // BLK
    spread_ref[...] = exact_dot(sums[...], (left == right).astype(F32))
    block = lax.broadcasted_iota(jnp.int32, (8, LANES), 0)
    pick = (block == column // BLK).astype(F32)
    for half in range(2):
        coarse_ref[half * 8 : half * 8 + 8, :] = lax.dot_general(
            pick,
            sums[half * NNULL : (half + 1) * NNULL, :],
            (((1,), (1,)), ((), ())),
            precision=lax.Precision.HIGHEST,
            preferred_element_type=F32,
        )

    scale = 2.0 / (ROWS * LANES * nt * nz * ny)

    def prolong_step(j, carry):
        re = miss[pl.ds(pl.multiple_of(j * ROWS, ROWS), ROWS), :]
        im = miss[pl.ds(pl.multiple_of((12 + j) * ROWS, ROWS), ROWS), :]
        for k in range(NNULL):
            v_re = null_ref[pl.ds(pl.multiple_of((k * 24 + j) * ROWS, ROWS), ROWS), :].astype(F32)
            v_im = null_ref[
                pl.ds(pl.multiple_of((k * 24 + 12 + j) * ROWS, ROWS), ROWS), :
            ].astype(F32)
            s_re = spread_ref[k : k + 1, :]
            s_im = spread_ref[NNULL + k : NNULL + k + 1, :]
            re = re + (s_re * v_re - s_im * v_im)
            im = im + (s_re * v_im + s_im * v_re)
        cot[pl.ds(pl.multiple_of(j * ROWS, ROWS), ROWS), :] = re * scale
        cot[pl.ds(pl.multiple_of((12 + j) * ROWS, ROWS), ROWS), :] = im * scale
        return carry

    lax.fori_loop(0, 12, prolong_step, 0)

    load_source(cot)
    identity_path()
    exchange(3, from_field, from_field, put_swapped)

    def back_step(t, carry):
        first_sum, second_sum = carry
        columns = stacked_columns(t)
        result = dot(back_ref[...], columns)
        back = split(result[0:16] + result[16:32])
        first_cols = x_first[t]
        g1 = dot_t(back, first_cols[0:STACK]) + dot_t(back, first_cols[STACK : 2 * STACK])
        g2 = dot_t(hid[t], columns[0:STACK]) + dot_t(hid[t], columns[STACK : 2 * STACK])
        return first_sum + g1[0:16] + g1[16:32], second_sum + g2[0:16] + g2[16:32]

    zero = jnp.zeros((16, STACK), F32)
    first_sum, second_sum = lax.fori_loop(0, LT, back_step, (zero, zero), unroll=True)

    grad_ref[...] = jnp.zeros_like(grad_ref)
    grad_ref[0:16, 0:STACK] = first_sum
    grad_ref[16:32, 0:STACK] = second_sum
    base = 0
    for partners, mine, slots in ((plane, iz * ny + iy, red_y), (column_of, it, red_t)):
        slots[mine] = grad_ref[...]
        copies = []
        for step, partner in enumerate(partners):
            copy = pltpu.make_async_remote_copy(
                src_ref=slots.at[mine],
                dst_ref=slots.at[mine],
                send_sem=red_send.at[base + step],
                recv_sem=red_recv.at[base + step],
                device_id=partner,
                device_id_type=MESH,
            )
            copy.start()
            copies.append(copy)
        for copy in copies:
            copy.wait()
        acc = slots[0]
        for j in range(1, len(partners) + 1):
            acc = acc + slots[j]
        grad_ref[...] = acc
        base += len(partners)
    weight_ref[...] = gather_weights(grad_ref[:, 0:STACK])


def store_kernel(out_ref, coarse_ref, weight_ref, out_hbm, coarse_hbm, first_hbm, second_hbm, sem):
    pairs = [
        (out_ref, out_hbm),
        (coarse_ref, coarse_hbm),
        (weight_ref.at[0:64, :], first_hbm),
        (weight_ref.at[64:128, :], second_hbm),
    ]
    copies = [pltpu.make_async_copy(src, dst, sem.at[k]) for k, (src, dst) in enumerate(pairs)]
    for copy in copies:
        copy.start()
    for copy in copies:
        copy.wait()


def body(sizes, source, gauge_links, near_null, w_first, w_second):
    nt, nz, ny = sizes
    vmem = pl.BlockSpec(memory_space=pltpu.VMEM)
    slab = (3, 8, LANES)
    hbm = pl.BlockSpec(memory_space=pltpu.HBM)
    out, coarse, grad = pl.pallas_call(
        functools.partial(kernel, sizes),
        out_shape=(
            jax.ShapeDtypeStruct((24 * ROWS, LANES), F32),
            jax.ShapeDtypeStruct((16, NNULL), F32),
            jax.ShapeDtypeStruct((128, 9), F32),
        ),
        in_specs=[hbm] * 6,
        out_specs=(vmem, vmem, vmem),
        scratch_shapes=[
            pltpu.VMEM((24 * ROWS, LANES), F32),
            pltpu.VMEM((72 * ROWS, LANES), F32),
            pltpu.VMEM((NNULL * 24 * ROWS, LANES), BF16),
            pltpu.VMEM((2, 64, 9), F32),
            pltpu.VMEM((16, 2 * STACK), F32),
            pltpu.VMEM((32, 2 * STACK), BF16),
            pltpu.VMEM((2 * STACK, 32), BF16),
            pltpu.VMEM((32, 2 * STACK), BF16),
            pltpu.VMEM((32, LANES), F32),
            pltpu.VMEM((4, 6, 4) + slab, F32),
            pltpu.VMEM((4, 6, 4) + slab, F32),
            pltpu.VMEM((LT, LZ) + slab, F32),
            pltpu.VMEM((LT, LZ) + slab, F32),
            pltpu.VMEM((LT, LZ, 3, STACK, LANES), F32),
            pltpu.VMEM((LT, 2 * STACK, WIDE), BF16),
            pltpu.VMEM((LT, 32, WIDE), BF16),
            pltpu.VMEM((LT, LZ, 3, STACK, LANES), F32),
            pltpu.VMEM((LT, LZ) + slab, F32),
            pltpu.VMEM((24 * ROWS, LANES), F32),
            pltpu.VMEM((24 * ROWS, LANES), F32),
            pltpu.VMEM((2 * NNULL, LANES), F32),
            pltpu.VMEM((2 * NNULL, LANES), F32),
            pltpu.VMEM((ny * nz, 32, LANES), F32),
            pltpu.VMEM((nt, 32, LANES), F32),
            pltpu.SemaphoreType.DMA((4, 6)),
            pltpu.SemaphoreType.DMA((4, 6)),
            pltpu.SemaphoreType.DMA((nt + nz * ny,)),
            pltpu.SemaphoreType.DMA((nt + nz * ny,)),
            pltpu.SemaphoreType.DMA((9,)),
        ],
        compiler_params=pltpu.CompilerParams(
            collective_id=0, has_side_effects=True, vmem_limit_bytes=(65536 - 288) * 1024
        ),
    )(
        source.reshape(24 * ROWS, LANES),
        gauge_links.reshape(72 * ROWS, LANES),
        near_null.reshape(NNULL * 24 * ROWS, LANES),
        jnp.transpose(w_first, (1, 2, 3, 4, 5, 0)).reshape(64, 9),
        jnp.transpose(w_second, (1, 2, 3, 4, 5, 0)).reshape(64, 9),
        jnp.asarray(dirac_matrix()),
    )
    out, coarse, first, second = pl.pallas_call(
        store_kernel,
        out_shape=(
            jax.ShapeDtypeStruct((24 * ROWS, LANES), F32),
            jax.ShapeDtypeStruct((16, NNULL), F32),
            jax.ShapeDtypeStruct((64, 9), F32),
            jax.ShapeDtypeStruct((64, 9), F32),
        ),
        in_specs=[vmem] * 3,
        out_specs=(hbm,) * 4,
        scratch_shapes=[pltpu.SemaphoreType.DMA((4,))],
    )(out, coarse, grad)

    def as_weights(values, outs, ins):
        return jnp.transpose(values.reshape(outs, ins, 2, 4, 4, 9), (5, 0, 1, 2, 3, 4))

    return (
        out.reshape(source.shape),
        jnp.transpose(coarse.reshape(2, 1, 1, LX // BLK, NNULL), (0, 4, 1, 2, 3)),
        as_weights(first, 2, 1),
        as_weights(second, 1, 2),
    )


def solution(mesh):
    sizes = (mesh.shape["ta"], mesh.shape["gz"], mesh.shape["gy"])
    in_specs = (
        P(None, None, None, "ta", "gz", "gy"),
        P(None, None, None, None, "ta", "gz", "gy"),
        P(None, None, None, None, "ta", "gz", "gy"),
        P(),
        P(),
    )
    out_specs = (P(None, None, None, "ta", "gz", "gy"), P(None, None, "ta", "gz", "gy"), P(), P())
    return jax.shard_map(
        functools.partial(body, sizes),
        mesh=mesh,
        in_specs=in_specs,
        out_specs=out_specs,
        check_vma=False,
    )
```
